128 devices in a mesh: fsdp: 4 (over z), expert: 32 (over x, y, core).
Axes of the slice: x: 4, y: 4, z: 4, core: 2. Of those that a mesh axis runs over, the one named last changes fastest.
Arguments:
- inputs: bfloat16 [4, 2048, 2048], P(None, ('fsdp', 'expert')), may hold values from -6 to 6
- cache_keys: bfloat16 [2048, 128, 256], P(('fsdp', 'expert'))
- cache_values: bfloat16 [2048, 128, 256], P(('fsdp', 'expert')), may hold values from -6 to 6
- lengths: int32 [2048], P(('fsdp', 'expert')), may hold values from 2 to 128, as said below
- new_keys: bfloat16 [4, 2048, 256], P(None, ('fsdp', 'expert')), may hold values from -6 to 6
- new_values: bfloat16 [4, 2048, 256], P(None, ('fsdp', 'expert')), may hold values from -6 to 6
- queries: bfloat16 [4, 2048, 2048], P(None, ('fsdp', 'expert'))
- out_weight: bfloat16 [2048, 2048], P('fsdp'), may hold values from -0.125 to 0.125
- norm_gain: bfloat16 [2048], replicated, may hold values from 0.099609375 to 1.8984375
- router: bfloat16 [2048, 128], replicated
- experts: int32 [4, 2048, 8], P(None, ('fsdp', 'expert')), may hold values from 0 to 127, all different within a row; in each aligned block of 16 rows (0 to 15, 16 to 31, ..., all dimensions but the last counted through in order) at most 2 rows name the same one
- master_gate: float32 [128, 2048, 768], P('fsdp', 'expert'), may hold values from -0.125 to 0.125
- master_up: float32 [128, 2048, 768], P('fsdp', 'expert'), may hold values from -0.125 to 0.125
- master_down: float32 [128, 2048, 768], P('fsdp', 'expert'), may hold values from -0.4375 to 0.4375
Outputs:
- outputs: bfloat16 [4, 2048, 2048], P(None, ('fsdp', 'expert'))
The draws below stay inside these ranges and needn't reach their ends.
Inputs may be any that keep to these rules, and one draw needn't show every extreme that they name: Each row names 8 different experts. In each step the 16 rows of one device name any one expert at most 2 times, a bound that some block reaches by one device's rows. `lengths`: some row has a full cache.
All inputs are finite; a program needn't handle non-finite values.
Results may differ from the reference program's by a relative error of at most 0.006.
Values may be sent and summed in bfloat16 or wider, within the bound.
A program may use at most 128 MiB of HBM per device.

```python
import math
import jax
import jax.numpy as jnp
import numpy as np
from jax import lax

D = 2048
FF = 768
HEAD_DIM = 128
Q_HEADS = 16
KV_HEADS = 2
TOP = 8
STEPS = 4
R_DEV = 16
CACHE_LEN = 128
GROUP = 8
EXPERTS = 128
ROWS = 2048
CAP = 2


def shared_keys(key):
    return jax.random.normal(key, (ROWS, CACHE_LEN, KV_HEADS * HEAD_DIM), jnp.float32)


def draw_cache_keys(key, part):
    return shared_keys(key).astype(jnp.bfloat16)


def draw_queries(key, part):
    key = jax.random.fold_in(key, 5)
    key_fresh = jax.random.fold_in(key, 0)
    whole = jax.random.normal(key_fresh, (STEPS, ROWS, KV_HEADS, GROUP, HEAD_DIM), jnp.float32)
    return whole.reshape(STEPS, ROWS, Q_HEADS * HEAD_DIM).astype(jnp.bfloat16)


def draw_router(key, part):
    key = jax.random.fold_in(key, 9)
    key_body = jax.random.fold_in(key, 0)
    weights = 0.35 * jax.random.normal(key_body, (D, EXPERTS), jnp.float32)
    return (weights * D ** (-0.5)).astype(jnp.bfloat16)


def draw_lengths(key, part):
    key = jax.random.fold_in(key, 11)
    drawn = jax.random.randint(key, (ROWS,), 2, CACHE_LEN + 1)
    return drawn.at[0].set(CACHE_LEN).astype(jnp.int32)


def block_levels(key, shape, shards, smallest, top_value):
    def one(dim, blocks):
        steps = jax.random.uniform(jax.random.fold_in(jax.random.fold_in(key, 6), dim), (blocks,), jnp.float32, smallest / len(shards), top_value / len(shards))
        return jnp.repeat(jnp.exp(steps), shape[dim] // blocks).reshape((-1,) + (1,) * (len(shape) - dim - 1))

    gain = one(*shards[0])
    for cut in shards[1:]:
        gain = gain * one(*cut)
    return gain


def deal_out(rng, own, number, rows, amount, top, limit, skew):
    order = jax.random.permutation(rng, amount)
    crowded, ordinary = shares(amount, rows * top, limit, skew, True), shares(amount, rows * top, limit, skew, False)
    places = jnp.arange(amount)

    def named(sizes, offset_by):
        used = int((sizes > 0).sum())
        fixed = max(1, used // 4)
        passed = fixed + (places - fixed + offset_by * (used - fixed)) % max(1, amount - fixed)
        return jnp.zeros((amount,), jnp.int32).at[order[jnp.where(places < fixed, places, passed)]].set(jnp.asarray(sizes, jnp.int32))

    sizes = jnp.where(number % 4 == 0, named(crowded, number // 4), named(ordinary, number - number // 4 - 1))
    mixed = jax.random.permutation(jax.random.fold_in(own, 3), amount)
    donor, receiver = mixed[0:amount // 2 * 2:2], mixed[1:amount // 2 * 2:2]
    slack = jnp.minimum(sizes[donor] - 1, limit - sizes[receiver]) // 2
    slack = jnp.where((donor == order[0]) | (receiver == order[0]) | (sizes[receiver] == 0), 0, jnp.maximum(slack, 0))
    passed = jax.random.randint(jax.random.fold_in(own, 4), (amount // 2,), 0, 1 << 20) % (slack + 1)
    sizes = sizes.at[donor].add(-passed).at[receiver].add(passed)
    labels = jnp.searchsorted(jnp.cumsum(sizes), jnp.arange(rows * top), side="right").astype(jnp.int32)
    grid = labels.reshape(top, rows).T
    grid = grid[jax.random.permutation(jax.random.fold_in(own, 1), rows)]
    offset_by = jax.random.randint(jax.random.fold_in(own, 2), (rows, 1), 0, top)
    return jnp.take_along_axis(grid, (jnp.arange(top)[None, :] + offset_by) % top, axis=1)


def shares(number_of, total, limit, slope, full):
    loads = [(1 << 20) // math.isqrt(grade ** slope) + 1 for grade in range(1, number_of + 1)]
    largest = limit if full else min(limit, max(-(-total // number_of), total * loads[0] // sum(loads)))
    least = 1 if total - largest >= number_of - 1 else 0
    holding, spare = [largest] + [least] * (number_of - 1), total - largest - least * (number_of - 1)
    while spare > 0:
        movable = [i for i in range(1, number_of) if holding[i] < largest] or [i for i in range(1, number_of) if holding[i] < limit]
        mass, budget = sum([loads[i] for i in movable]), spare
        for i in movable:
            addition = min(limit - holding[i], max(1, budget * loads[i] // mass), spare)
            holding[i] = holding[i] + addition
            spare = spare - addition
    return np.array(holding)


def bell_draw(stream_key, dims, deviation, reach, pieces=(), dtype=jnp.bfloat16):
    array = deviation * jax.random.normal(stream_key, dims, jnp.float32)
    if pieces:
        array = array * block_levels(stream_key, dims, pieces, -0.22, 0.18)
    return jnp.clip(array, -reach, reach).astype(dtype)


def setup_inputs(seed: int = 0) -> dict:
    splits = jax.random.split(jax.random.key(seed), 15)
    inputs = bell_draw(splits[0], (STEPS, ROWS, D), 1.0, 6.0, ((1, 128),))
    cache_keys = draw_cache_keys(jax.random.fold_in(splits[14], 71), 0)
    cache_values = bell_draw(splits[2], (ROWS, CACHE_LEN, KV_HEADS * HEAD_DIM), 1.0, 6.0, ((0, 128),))
    lengths = draw_lengths(jax.random.fold_in(splits[14], 71), 0)
    new_keys = bell_draw(splits[4], (STEPS, ROWS, KV_HEADS * HEAD_DIM), 1.0, 6.0, ((1, 128),))
    new_values = bell_draw(splits[5], (STEPS, ROWS, KV_HEADS * HEAD_DIM), 1.0, 6.0, ((1, 128),))
    queries = draw_queries(jax.random.fold_in(splits[14], 71), 0)
    out_weight = bell_draw(splits[7], (Q_HEADS * HEAD_DIM, D), (Q_HEADS * HEAD_DIM) ** -0.5, 0.125, ((0, 4),))
    norm_gain = jnp.clip(1.0 + 0.18 * jax.random.normal(splits[8], (D,), jnp.float32), 0.099609375, 1.8984375).astype(jnp.bfloat16)
    router = draw_router(jax.random.fold_in(splits[14], 71), 0)
    experts_keys = jax.random.split(jax.random.fold_in(splits[10], 1), STEPS * ROWS // R_DEV)
    experts_turns = jax.random.permutation(jax.random.fold_in(splits[10], 3), STEPS * ROWS // R_DEV)
    experts = jax.vmap(lambda own, number: deal_out(jax.random.fold_in(splits[10], 2), own, number, R_DEV, EXPERTS, TOP, CAP, 2))(experts_keys, experts_turns).reshape((STEPS, ROWS, TOP))
    master_gate = bell_draw(splits[11], (EXPERTS, D, FF), D ** -0.5, 0.125, ((0, 4), (1, 32)), jnp.float32)
    master_up = bell_draw(splits[12], (EXPERTS, D, FF), D ** -0.5, 0.125, ((0, 4), (1, 32)), jnp.float32)
    master_down = bell_draw(splits[13], (EXPERTS, D, FF), (FF // 4) ** -0.5, 0.4375, ((0, 4), (1, 32)), jnp.float32)
    return dict(inputs=inputs, cache_keys=cache_keys, cache_values=cache_values, lengths=lengths, new_keys=new_keys, new_values=new_values, queries=queries, out_weight=out_weight, norm_gain=norm_gain, router=router, experts=experts, master_gate=master_gate, master_up=master_up, master_down=master_down)


def expert_block(token_rows, w_gate, w_up, w_down):
    gate_part = jnp.dot(token_rows, w_gate, preferred_element_type=jnp.float32)
    up_part = jnp.dot(token_rows, w_up, preferred_element_type=jnp.float32)
    hidden = (jax.nn.silu(gate_part) * up_part).astype(jnp.bfloat16)
    product = lax.dot_general(hidden, w_down, (((1,), (1,)), ((), ())), preferred_element_type=jnp.float32)
    return product.astype(jnp.bfloat16)

def attend_rows(query_rows, cache_k, cache_v, fresh_k, fresh_v, valid_mask):
    inv_scale = 1.0 / math.sqrt(HEAD_DIM)
    cached = jnp.einsum('rgqd,rlgd->rgql', query_rows, cache_k) * inv_scale
    cached = jnp.where(valid_mask[:, None, None, :], cached, -jnp.inf)
    fresh = jnp.einsum('rgqd,srgd->rgqs', query_rows, fresh_k) * inv_scale
    scores = jnp.concatenate([cached, fresh], axis=-1)
    top_score = lax.optimization_barrier(jnp.max(scores, axis=-1, keepdims=True))
    expo = jnp.exp(scores - top_score)
    weights = (expo / lax.optimization_barrier(jnp.sum(expo, axis=-1, keepdims=True))).astype(jnp.bfloat16)
    values = jnp.concatenate([cache_v, jnp.transpose(fresh_v, (1, 0, 2, 3))], axis=1)
    mixed = jnp.einsum('rgql,rlgd->rgqd', weights.astype(jnp.float32), values)
    return mixed.reshape(mixed.shape[0], -1).astype(jnp.bfloat16)

def reference(inputs, cache_keys, cache_values, lengths, new_keys, new_values, queries, out_weight, norm_gain, router, experts, master_gate, master_up, master_down):
    cache_k = cache_keys.astype(jnp.float32).reshape(ROWS, CACHE_LEN, KV_HEADS, HEAD_DIM)
    cache_v = cache_values.astype(jnp.float32).reshape(ROWS, CACHE_LEN, KV_HEADS, HEAD_DIM)
    positions = jnp.arange(CACHE_LEN).astype(jnp.int32)
    valid_mask = positions[None, :] < lengths[:, None]
    normed_list = []
    resid_list = []
    for step_index in range(STEPS):
        query_rows = queries[step_index].astype(jnp.float32).reshape(ROWS, KV_HEADS, GROUP, HEAD_DIM)
        fresh_k = new_keys[:step_index + 1].astype(jnp.float32).reshape(step_index + 1, ROWS, KV_HEADS, HEAD_DIM)
        fresh_v = new_values[:step_index + 1].astype(jnp.float32).reshape(step_index + 1, ROWS, KV_HEADS, HEAD_DIM)
        attended = attend_rows(query_rows, cache_k, cache_v, fresh_k, fresh_v, valid_mask)
        resid = inputs[step_index].astype(jnp.float32) + jnp.dot(attended, out_weight, preferred_element_type=jnp.float32)
        mean_square = lax.optimization_barrier(jnp.mean(resid * resid, axis=-1, keepdims=True))
        normed = (resid * lax.rsqrt(mean_square + 1e-06) * norm_gain.astype(jnp.float32)).astype(jnp.bfloat16)
        normed_list.append(normed)
        resid_list.append(resid)
    normed_all = jnp.concatenate(normed_list, axis=0)
    resid_all = jnp.concatenate(resid_list, axis=0)
    slot_total = STEPS * ROWS * TOP
    flat_ids = experts.reshape(-1).astype(jnp.int32)
    order = jnp.argsort(flat_ids, stable=True).astype(jnp.int32)
    counts = jnp.zeros((EXPERTS,), jnp.int32).at[flat_ids].add(1)
    starts = jnp.cumsum(counts) - counts
    padded = (counts + 127) // 128 * 128
    pad_end = jnp.cumsum(padded)
    pad_start = pad_end - padded
    sorted_ids = flat_ids[order]
    ranking = jnp.arange(slot_total).astype(jnp.int32) - starts[sorted_ids]
    target = pad_start[sorted_ids] + ranking
    block_count = slot_total // 128 + EXPERTS
    table = jnp.full((block_count * 128,), -1, jnp.int32).at[target].set(order)
    block_start = (jnp.arange(block_count) * 128).astype(jnp.int32)
    block_owner = jnp.minimum(lax.optimization_barrier(jnp.sum((pad_end[None, :] <= block_start[:, None]).astype(jnp.int32), axis=1)), EXPERTS - 1).astype(jnp.int32)

    def run_block(packed):
        slot_index, owner = packed
        token_rows = normed_all[jnp.maximum(slot_index, 0) // TOP]
        w_gate = master_gate[owner].astype(jnp.bfloat16)
        w_up = master_up[owner].astype(jnp.bfloat16)
        w_down = master_down[owner].astype(jnp.bfloat16)
        return expert_block(token_rows, w_gate, w_up, w_down)
    produced = lax.map(run_block, (table.reshape(block_count, 128), block_owner))
    safe_index = jnp.where(table >= 0, table, slot_total)
    slot_out = jnp.zeros((slot_total, D), jnp.bfloat16).at[safe_index].set(produced.reshape(-1, D), mode='drop')
    logits = jnp.dot(normed_all, router, preferred_element_type=jnp.float32)
    chosen = jnp.take_along_axis(logits, experts.reshape(-1, TOP), axis=1)
    chosen_top = lax.optimization_barrier(jnp.max(chosen, axis=-1, keepdims=True))
    chosen_exp = jnp.exp(chosen - chosen_top)
    gating = chosen_exp / lax.optimization_barrier(jnp.sum(chosen_exp, axis=-1, keepdims=True))
    mixture = lax.optimization_barrier(jnp.sum(gating[:, :, None] * slot_out.reshape(-1, TOP, D).astype(jnp.float32), axis=1))
    return (resid_all + mixture).astype(jnp.bfloat16).reshape(STEPS, ROWS, D)
```

```python
import functools
import math

import jax
import jax.numpy as jnp
from jax import lax
from jax.experimental import pallas as pl
from jax.experimental.pallas import tpu as pltpu
from jax.sharding import PartitionSpec as P

MESH = pl.DeviceIdType.MESH
BF = jnp.bfloat16
F32 = jnp.float32
NT = (((1,), (1,)), ((), ()))
TN = (((0,), (0,)), ((), ()))
DEPTH = 8


def dot(a, b):
    return jnp.dot(a, b, preferred_element_type=F32)


def dot_nt(a, b):
    return lax.dot_general(a, b, NT, preferred_element_type=F32)


def dot_tn(a, b):
    return lax.dot_general(a, b, TN, preferred_element_type=F32)


def kernel(
    x_ref, q_ref, ck_ref, cv_ref, nk_ref, nv_ref, len_ref, gain_ref, router_ref, ids_ref,
    wo_ref, mg_ref, mu_ref, md_ref,
    out_ref,
    stage, ws, mid_a, mid_b, wgu, wd, wout, ag_a, ag_b, ssend, srecv,
    o_s, att, resid, pg, rs1, rs2, mix,
    st_sem, w1_s, w1_r, w2_s, w2_r, d2_s, d2_r, own_sem, o_snd, o_rcv, f_snd, f_rcv,
    ag_s, ag_r, z_s, z_r, t_s, t_r, r1_s, r1_r, r2_s, r2_r,
):
    z = lax.axis_index("fsdp")
    e = lax.axis_index("expert")
    x = e // 8
    y = (e // 2) % 4
    c = e % 2
    me = z * 2 + c

    def dev(dx=0, dy=0, dc=0, dz=0):
        return (
            (z + dz) % 4,
            ((x + dx) % 4) * 8 + ((y + dy) % 4) * 2 + (c + dc) % 2,
        )

    def remote(src, dst, snd, rcv, target):
        return pltpu.make_async_remote_copy(
            src_ref=src, dst_ref=dst, send_sem=snd, recv_sem=rcv,
            device_id=target, device_id_type=MESH,
        )

    masters = (mg_ref, mu_ref, md_ref)

    def load(t, j, slot):
        return pltpu.make_async_copy(masters[t].at[j // 4, j % 4], stage.at[slot], st_sem.at[slot])

    for j in range(DEPTH):
        load(0, j, j).start()
    own_out = pltpu.make_async_copy(wo_ref, wout.at[pl.ds(z * 4, 4)], own_sem)
    own_out.start()

    partners = [(d, 0, k, 0) for d in (1, 2, 3) for k in (0, 1)]
    partners += [(0, d, k, 0) for d in (1, 2, 3) for k in (0, 1)]
    partners += [(0, 0, k, d) for d in (1, 2, 3) for k in (0, 1)]
    partners += [(0, 0, 1, 0)]
    barrier = pltpu.get_barrier_semaphore()
    for p in partners:
        pl.semaphore_signal(barrier, inc=1, device_id=dev(*p), device_id_type=MESH)
    pl.semaphore_wait(barrier, len(partners))

    drains = []

    gathers = []
    for dz in (1, 2, 3):
        cp = remote(
            wo_ref.at[pl.ds(c * 2, 2)], wout.at[pl.ds(z * 4 + c * 2, 2)],
            o_snd.at[dz - 1], o_rcv.at[dz - 1], dev(dz=dz),
        )
        cp.start()
        gathers.append(cp)

    first = []
    for t in range(3):
        def cast(j, slot_t):
            slot = j % DEPTH
            load(t, j, slot).wait()
            ws[t, j // 4, j % 4] = stage[slot].astype(BF)
            return slot

        def step_a(j, carry):
            slot = cast(j, t)
            load(t, j + DEPTH, slot).start()
            return carry

        def step_b(j, carry):
            slot = cast(j, t)
            if t < 2:
                load(t + 1, j - DEPTH, slot).start()
            return carry

        lax.fori_loop(0, 16 - DEPTH, step_a, 0)
        lax.fori_loop(16 - DEPTH, 16, step_b, 0)
        group = []
        for d in (1, 3, 2, 0):
            for dc in (0, 1):
                i = d * 2 + dc
                xd, yd, cd = (x + d) % 4, (y + d) % 4, (c + dc) % 2
                src_a = ws.at[t, xd, :, cd, :, pl.ds(0, 384)]
                src_b = ws.at[t, :, yd, cd, :, pl.ds(384, 384)]
                if i == 0:
                    cp_a = pltpu.make_async_copy(src_a, mid_a.at[t, x, c], w1_r.at[t, 0, i])
                    cp_b = pltpu.make_async_copy(src_b, mid_b.at[t, y, c], w1_r.at[t, 1, i])
                else:
                    cp_a = remote(
                        src_a, mid_a.at[t, x, c], w1_s.at[t, 0, i], w1_r.at[t, 0, i],
                        dev(dx=d, dc=dc),
                    )
                    cp_b = remote(
                        src_b, mid_b.at[t, y, c], w1_s.at[t, 1, i], w1_r.at[t, 1, i],
                        dev(dy=d, dc=dc),
                    )
                    drains += [cp_a, cp_b]
                cp_a.start()
                cp_b.start()
                group += [(i, cp_a), (i, cp_b)]
        first.append(group)

    def wait_group(group):
        for i, cp in group:
            if i == 0:
                cp.wait()
            else:
                cp.wait_recv()

    def second(t, k):
        group = []
        for d in (1, 3, 2, 0):
            xd, yd = (x + d) % 4, (y + d) % 4
            if k is None:
                src_a, src_b = mid_a.at[t, :, :, yd], mid_b.at[t, :, :, xd]
                dst_a = wgu.at[t, :, y, :, :, pl.ds(0, 384)]
                dst_b = wgu.at[t, x, :, :, :, pl.ds(384, 384)]
                snd, rcv = w2_s.at[t], w2_r.at[t]
            else:
                src_a = mid_a.at[t, :, :, yd, pl.ds(16 * k, 16)]
                src_b = mid_b.at[t, :, :, xd, pl.ds(16 * k, 16)]
                dst_a = wd.at[k, :, y, :, :, pl.ds(0, 384)]
                dst_b = wd.at[k, x, :, :, :, pl.ds(384, 384)]
                snd, rcv = d2_s.at[k], d2_r.at[k]
            if d == 0:
                cp_a = pltpu.make_async_copy(src_a, dst_a, rcv.at[0, 0])
                cp_b = pltpu.make_async_copy(src_b, dst_b, rcv.at[1, 0])
            else:
                cp_a = remote(src_a, dst_a, snd.at[0, d], rcv.at[0, d], dev(dy=d))
                cp_b = remote(src_b, dst_b, snd.at[1, d], rcv.at[1, d], dev(dx=d))
                drains.extend([cp_a, cp_b])
            cp_a.start()
            cp_b.start()
            group += [(d, cp_a), (d, cp_b)]
        return group

    inv = 1.0 / math.sqrt(128.0)
    neg = -jnp.inf
    lane = lax.broadcasted_iota(jnp.int32, (32, 128), 1)
    fresh_ok = lax.broadcasted_iota(jnp.int32, (32, 16), 1) <= (
        lax.broadcasted_iota(jnp.int32, (32, 16), 0) >> 3
    )

    def attend(r, carry):
        ok = lane < len_ref[r]
        for g in range(2):
            cols = slice(g * 128, (g + 1) * 128)
            qq = q_ref[r, g]
            s = jnp.where(ok, dot_nt(qq, ck_ref[r, :, cols]) * inv, neg)
            f = jnp.where(fresh_ok, dot_nt(qq, nk_ref[r, :, cols]) * inv, neg)
            top = jnp.maximum(
                jnp.max(s, axis=-1, keepdims=True), jnp.max(f, axis=-1, keepdims=True)
            )
            es, ef = jnp.exp(s - top), jnp.exp(f - top)
            total = jnp.sum(es, axis=-1, keepdims=True) + jnp.sum(ef, axis=-1, keepdims=True)
            ps, pf = (es / total).astype(BF), (ef / total).astype(BF)
            o_s[r, g] = dot(ps, cv_ref[r, :, cols]) + dot(pf, nv_ref[r, :, cols])
        return carry

    lax.fori_loop(0, 16, attend, 0)
    for g in range(2):
        for h in range(8):
            for t in range(4):
                head = g * 8 + h
                att[t * 16:(t + 1) * 16, head * 128:(head + 1) * 128] = o_s[
                    :, g, t * 8 + h, :
                ].astype(BF)

    forwards = []
    for dz in (1, 2, 3):
        gathers[dz - 1].wait_recv()
        part = wout.at[pl.ds(((z + 4 - dz) % 4) * 4 + c * 2, 2)]
        cp = remote(part, part, f_snd.at[dz - 1], f_rcv.at[dz - 1], dev(dc=1))
        cp.start()
        forwards.append(cp)
    wait_group(first[0])
    g2 = second(0, None)
    own_out.wait()
    for cp in gathers:
        cp.wait_send()
    for cp in forwards:
        cp.wait()

    def project(n, carry):
        cols = pl.ds(pl.multiple_of(n * 512, 512), 512)
        w = wout[:, :, :, cols].reshape(2048, 512)
        resid[:, cols] = x_ref[:, cols].astype(F32) + dot(att[...], w)
        return carry

    lax.fori_loop(0, 4, project, 0)
    res = resid[...]
    mean_square = jnp.mean(res * res, axis=-1, keepdims=True)
    normed = (res * lax.rsqrt(mean_square + 1e-06) * gain_ref[...].astype(F32)).astype(BF)
    ag_a[y, x, :, 0:1024] = normed[:, 0:1024]
    ag_b[x, y] = normed[:, 1024:2048]
    logits = dot(normed, router_ref[...])
    column = lax.broadcasted_iota(jnp.int32, (64, 128), 1)
    member = jnp.zeros((64, 128), F32)
    for k in range(8):
        member = member + (ids_ref[:, k:k + 1] == column).astype(F32)
    row_i = lax.broadcasted_iota(jnp.int32, (64, 64), 0)
    col_i = lax.broadcasted_iota(jnp.int32, (64, 64), 1)
    before = ((row_i >> 4) == (col_i >> 4)) & (col_i < row_i)
    rank = dot(before.astype(F32).astype(BF), member.astype(BF))
    chosen = jnp.where(member > 0.5, logits, neg)
    chosen_exp = jnp.exp(chosen - jnp.max(chosen, axis=-1, keepdims=True))
    gates = chosen_exp / jnp.sum(chosen_exp, axis=-1, keepdims=True)
    ag_a[y, x, :, 1024:1152] = jnp.where(rank < 0.5, gates, -gates).astype(BF)

    ag1 = []
    for d in (1, 3, 2):
        cp_a = remote(
            ag_a.at[y, x], ag_a.at[y, x], ag_s.at[0, d], ag_r.at[0, d], dev(dx=d)
        )
        cp_b = remote(
            ag_b.at[x, y], ag_b.at[x, y], ag_s.at[1, d], ag_r.at[1, d], dev(dy=d)
        )
        cp_a.start()
        cp_b.start()
        ag1 += [cp_a, cp_b]
    wait_group(first[1])
    u2 = second(1, None)
    for cp in ag1:
        cp.wait()
    ag2 = []
    for d in (1, 3, 2):
        cp_a = remote(ag_a.at[y], ag_a.at[y], ag_s.at[2, d], ag_r.at[2, d], dev(dy=d))
        cp_b = remote(ag_b.at[x], ag_b.at[x], ag_s.at[3, d], ag_r.at[3, d], dev(dx=d))
        cp_a.start()
        cp_b.start()
        ag2 += [cp_a, cp_b]
    wait_group(first[2])
    d2 = [second(2, k) for k in range(4)]
    for cp in ag2:
        cp.wait()

    e_row = lax.broadcasted_iota(jnp.int32, (8, 128), 0)
    e_lane = lax.broadcasted_iota(jnp.int32, (8, 128), 1)
    pick = (e_lane == (e_row >> 1) * 32 + (e_row & 1) + x * 8 + y * 2).astype(F32).astype(BF)
    slot_i = lax.broadcasted_iota(jnp.int32, (8, 32, 256), 1)
    row_of = lax.broadcasted_iota(jnp.int32, (8, 32, 256), 2)
    same = (row_of >> 4) == (slot_i >> 1)
    sign = jnp.where((slot_i & 1) == 0, 1.0, -1.0).astype(F32)

    def select(t, carry):
        rows = pl.ds(pl.multiple_of(t * 16, 16), 16)
        dst = pl.ds(pl.multiple_of((t % 2) * 32, 32), 32)
        aux = ag_a[:, :, rows, 1024:1152].reshape(256, 128)
        code = dot_nt(pick, aux)
        signed = jnp.where(same, code[:, None, :] * sign, 0.0)
        weight = jnp.maximum(signed, 0.0).reshape(256, 256)
        pg[t] = weight.astype(BF)
        place = (weight > 0.0).astype(F32).astype(BF)
        for n in range(2):
            cols = slice(n * 512, (n + 1) * 512)
            got = dot(place, ag_a[:, :, rows, cols].reshape(256, 512))
            ssend[:, t // 2, dst, cols] = got.astype(BF).reshape(8, 32, 512)
        for n in range(2):
            cols = slice(n * 512, (n + 1) * 512)
            part = jnp.concatenate(
                [ag_b[:, k, rows, cols].reshape(64, 512) for k in range(4)], axis=0
            )
            got = dot(place, part)
            ssend[:, t // 2, dst, n * 512 + 1024:n * 512 + 1536] = got.astype(BF).reshape(8, 32, 512)
        return carry

    lax.fori_loop(0, 4, select, 0)

    column_devs = [(dz, dc) for dz in (1, 3, 2, 0) for dc in (0, 1)]
    dispatch = []
    for dz, dc in column_devs:
        i = dz * 2 + dc
        to = ((z + dz) % 4) * 2 + (c + dc) % 2
        if i == 0:
            cp = pltpu.make_async_copy(ssend.at[me], srecv.at[me], z_r.at[i])
        else:
            cp = remote(ssend.at[to], srecv.at[me], z_s.at[i], z_r.at[i], dev(dz=dz, dc=dc))
        cp.start()
        dispatch.append(cp)
    wait_group(g2)
    wait_group(u2)
    for cp in dispatch:
        cp.wait()

    def hide(i, carry):
        rows = srecv[pl.ds(i * 2, 2)].reshape(256, 2048)
        gate = dot(rows, wgu[0].reshape(2048, 768))
        up = dot(rows, wgu[1].reshape(2048, 768))
        ag_b[i, :, :, 0:768] = (jax.nn.silu(gate) * up).astype(BF).reshape(4, 64, 768)
        return carry

    lax.fori_loop(0, 4, hide, 0)

    def down(k):
        cols = slice(k * 512, (k + 1) * 512)
        wait_group(d2[k])

        def tile(i, carry):
            hidden = ag_b[i, :, :, 0:768].reshape(256, 768)
            got = dot_nt(hidden, wd[k].reshape(512, 768))
            srecv[pl.ds(i * 2, 2), :, :, cols] = got.astype(BF).reshape(2, 2, 64, 512)
            return carry

        lax.fori_loop(0, 4, tile, 0)
        group = []
        for dz, dc in column_devs:
            i = dz * 2 + dc
            to = ((z + dz) % 4) * 2 + (c + dc) % 2
            dst = wout.at[me, :, :, pl.ds(k * 512, 512)]
            if i == 0:
                cp = pltpu.make_async_copy(
                    srecv.at[me, :, :, pl.ds(k * 512, 512)], dst, t_r.at[k, i]
                )
            else:
                cp = remote(
                    srecv.at[to, :, :, pl.ds(k * 512, 512)], dst, t_s.at[k, i], t_r.at[k, i],
                    dev(dz=dz, dc=dc),
                )
                drains.append(cp)
            cp.start()
            group.append((i, cp))
        return group

    def combine(k, group):
        wait_group(group)

        def tile(t, carry):
            rows = pl.ds(pl.multiple_of(t * 16, 16), 16)
            src = pl.ds(pl.multiple_of((t % 2) * 32, 32), 32)
            got = wout[0:8, t // 2, src, k * 512:(k + 1) * 512].reshape(256, 512)
            part = dot_tn(pg[t], got).astype(BF)
            wout[8:16, :, rows, k * 512:k * 512 + 256] = part[:, 0:256].reshape(8, 2, 16, 256)
            for yy in range(4):
                for xx in range(4):
                    b = (yy * 4 + xx) * 16
                    wout[8 + xx * 2 + yy // 2, yy % 2, rows, k * 512 + 256:(k + 1) * 512] = part[
                        b:b + 16, 256:512
                    ]
            return carry

        lax.fori_loop(0, 4, tile, 0)
        sums = []
        for d in (1, 3, 2):
            xd, yd = (x + d) % 4, (y + d) % 4
            cp_a = remote(
                wout.at[pl.ds(8 + yd * 2, 2), :, :, pl.ds(k * 512, 256)], rs1.at[k, 0, d - 1],
                r1_s.at[k, 0, d - 1], r1_r.at[k, 0, d - 1], dev(dy=d),
            )
            cp_b = remote(
                wout.at[pl.ds(8 + xd * 2, 2), :, :, pl.ds(k * 512 + 256, 256)],
                rs1.at[k, 1, d - 1],
                r1_s.at[k, 1, d - 1], r1_r.at[k, 1, d - 1], dev(dx=d),
            )
            cp_a.start()
            cp_b.start()
            sums += [cp_a, cp_b]
        drains.extend(sums)
        return sums

    def halfway(k, sums):
        for cp in sums:
            cp.wait_recv()
        for route in range(2):
            mine = (y, x)[route]
            lanes = slice(k * 512 + route * 256, k * 512 + route * 256 + 256)
            total = wout[pl.ds(8 + mine * 2, 2), :, :, lanes].reshape(256, 256).astype(F32)
            for d in range(3):
                total = total + rs1[k, route, d].reshape(256, 256).astype(F32)
            ag_a[k, :, :, route * 256:(route + 1) * 256] = total.astype(BF).reshape(4, 64, 256)
        group = []
        for d in (1, 3, 2):
            xd, yd = (x + d) % 4, (y + d) % 4
            cp_a = remote(
                ag_a.at[k, xd, :, pl.ds(0, 256)], rs2.at[k, 0, d - 1],
                r2_s.at[k, 0, d - 1], r2_r.at[k, 0, d - 1], dev(dx=d),
            )
            cp_b = remote(
                ag_a.at[k, yd, :, pl.ds(256, 256)], rs2.at[k, 1, d - 1],
                r2_s.at[k, 1, d - 1], r2_r.at[k, 1, d - 1], dev(dy=d),
            )
            cp_a.start()
            cp_b.start()
            group += [cp_a, cp_b]
        drains.extend(group)
        return group

    def close(k, group):
        for cp in group:
            cp.wait_recv()
        for route in range(2):
            mine = (x, y)[route]
            total = ag_a[k, mine, :, route * 256:(route + 1) * 256].astype(F32)
            for d in range(3):
                total = total + rs2[k, route, d].astype(F32)
            mix[:, k * 512 + route * 256:k * 512 + (route + 1) * 256] = total

    backs, sums, ends = {}, {}, {}
    for k in range(7):
        if k < 4:
            backs[k] = down(k)
        if 0 <= k - 1 < 4:
            sums[k - 1] = combine(k - 1, backs[k - 1])
        if 0 <= k - 2 < 4:
            ends[k - 2] = halfway(k - 2, sums[k - 2])
        if 0 <= k - 3 < 4:
            close(k - 3, ends[k - 3])

    p_i = lax.broadcasted_iota(jnp.int32, (512, 512), 0)
    o_i = lax.broadcasted_iota(jnp.int32, (512, 512), 1)
    perm = (o_i == ((p_i >> 4) & 7) * 64 + (p_i >> 7) * 16 + (p_i & 15)).astype(F32).astype(BF)
    for g in range(4):
        v = jnp.concatenate(
            [mix[:, k * 512 + g * 128:k * 512 + (g + 1) * 128] for k in range(4)], axis=1
        )
        hi = v.astype(BF)
        lo = (v - hi.astype(F32)).astype(BF)
        out_ref[:, g * 512:(g + 1) * 512] = (
            resid[:, g * 512:(g + 1) * 512] + dot(hi, perm) + dot(lo, perm)
        )
    for cp in drains:
        cp.wait_send()


def per_device(
    inputs, cache_keys, cache_values, lengths, new_keys, new_values, queries, out_weight,
    norm_gain, router, experts, master_gate, master_up, master_down,
):
    q = queries.reshape(4, 16, 2, 8, 128).transpose(1, 2, 0, 3, 4).reshape(16, 2, 32, 128)
    nk = jnp.pad(new_keys.transpose(1, 0, 2), ((0, 0), (0, 12), (0, 0)))
    nv = jnp.pad(new_values.transpose(1, 0, 2), ((0, 0), (0, 12), (0, 0)))
    lens = jnp.broadcast_to(lengths[:, None, None], (16, 1, 128))
    vm = pl.BlockSpec(memory_space=pltpu.VMEM)
    anyspace = pl.BlockSpec(memory_space=pl.ANY)
    dma = pltpu.SemaphoreType.DMA
    shape5 = (4, 4, 2, 64, 768)
    out = pl.pallas_call(
        kernel,
        out_shape=jax.ShapeDtypeStruct((64, 2048), F32),
        in_specs=[vm] * 10 + [anyspace] * 4,
        out_specs=vm,
        scratch_shapes=[
            pltpu.VMEM((DEPTH, 2, 64, 768), F32),
            pltpu.VMEM((3, 4, 4, 2, 64, 768), BF),
            pltpu.VMEM((3, 4, 2, 4, 64, 384), BF),
            pltpu.VMEM((3, 4, 2, 4, 64, 384), BF),
            pltpu.VMEM((2, 4, 4, 2, 64, 768), BF),
            pltpu.VMEM((4, 4, 4, 2, 16, 768), BF),
            pltpu.VMEM((16, 2, 64, 2048), BF),
            pltpu.VMEM((4, 4, 64, 1152), BF),
            pltpu.VMEM((4, 4, 64, 1024), BF),
            pltpu.VMEM((8, 2, 64, 2048), BF),
            pltpu.VMEM((8, 2, 64, 2048), BF),
            pltpu.VMEM((16, 2, 32, 128), F32),
            pltpu.VMEM((64, 2048), BF),
            pltpu.VMEM((64, 2048), F32),
            pltpu.VMEM((4, 256, 256), BF),
            pltpu.VMEM((4, 2, 3, 2, 2, 64, 256), BF),
            pltpu.VMEM((4, 2, 3, 64, 256), BF),
            pltpu.VMEM((64, 2048), F32),
            dma((DEPTH,)),
            dma((3, 2, 8)), dma((3, 2, 8)),
            dma((2, 2, 4)), dma((2, 2, 4)),
            dma((4, 2, 4)), dma((4, 2, 4)),
            dma, dma((3,)), dma((3,)), dma((3,)), dma((3,)),
            dma((4, 4)), dma((4, 4)),
            dma((8,)), dma((8,)),
            dma((4, 8)), dma((4, 8)),
            dma((4, 2, 3)), dma((4, 2, 3)),
            dma((4, 2, 3)), dma((4, 2, 3)),
        ],
        compiler_params=pltpu.CompilerParams(
            collective_id=0, has_side_effects=True, vmem_limit_bytes=65_900_000
        ),
        name="moe_decode",
    )(
        inputs.reshape(64, 2048), q, cache_keys, cache_values, nk, nv, lens,
        norm_gain.reshape(1, 2048), router, experts.reshape(64, 8),
        out_weight.reshape(4, 2, 64, 2048),
        master_gate.reshape(shape5), master_up.reshape(shape5), master_down.reshape(shape5),
    )
    return out.astype(BF).reshape(4, 16, 2048)


def solution(mesh):
    return jax.shard_map(
        per_device,
        mesh=mesh,
        in_specs=(
            P(None, ("fsdp", "expert"), None),
            P(("fsdp", "expert"), None, None),
            P(("fsdp", "expert"), None, None),
            P(("fsdp", "expert")),
            P(None, ("fsdp", "expert"), None),
            P(None, ("fsdp", "expert"), None),
            P(None, ("fsdp", "expert"), None),
            P("fsdp", None),
            P(),
            P(),
            P(None, ("fsdp", "expert"), None),
            P("fsdp", "expert", None),
            P("fsdp", "expert", None),
            P("fsdp", "expert", None),
        ),
        out_specs=P(None, ("fsdp", "expert"), None),
        check_vma=False,
    )
```

```python
import functools
import math

import jax
import jax.numpy as jnp
from jax import lax
from jax.experimental import pallas as pl
from jax.experimental.pallas import tpu as pltpu
from jax.sharding import PartitionSpec as P

MESH = pl.DeviceIdType.MESH
BF = jnp.bfloat16
F32 = jnp.float32
NT = (((1,), (1,)), ((), ()))
TN = (((0,), (0,)), ((), ()))
DEPTH = 8
UNROLL = 4


def dot(a, b):
    return jnp.dot(a, b, preferred_element_type=F32)


def dot_nt(a, b):
    return lax.dot_general(a, b, NT, preferred_element_type=F32)


def dot_tn(a, b):
    return lax.dot_general(a, b, TN, preferred_element_type=F32)


def kernel(
    x_ref, q_ref, ck_ref, cv_ref, nk_ref, nv_ref, gain_ref, router_ref, ids_ref, len_ref,
    wo_ref, mg_ref, mu_ref, md_ref,
    out_ref,
    stage, ws, mid_a, mid_b, wgu, wd, wout, ag_a, ag_b, ssend, srecv,
    o_s, nk_s, nv_s, att, attr, resid, pg, rs1, rs2,
    st_sem, w1_s, w1_r, w2_s, w2_r, d2_s, d2_r, own_sem, o_snd, o_rcv, f_snd, f_rcv, one_sem,
    ag_s, ag_r, z_s, z_r, t_s, t_r, r1_s, r1_r, r2_s, r2_r,
):
    z = lax.axis_index("fsdp")
    e = lax.axis_index("expert")
    x = e // 8
    y = (e // 2) % 4
    c = e % 2
    me = z * 2 + c

    def dev(dx=0, dy=0, dc=0, dz=0):
        return (
            (z + dz) % 4,
            ((x + dx) % 4) * 8 + ((y + dy) % 4) * 2 + (c + dc) % 2,
        )

    def remote(src, dst, snd, rcv, target):
        return pltpu.make_async_remote_copy(
            src_ref=src, dst_ref=dst, send_sem=snd, recv_sem=rcv,
            device_id=target, device_id_type=MESH,
        )

    masters = (mg_ref, mu_ref, md_ref)

    def load(t, j, slot):
        return pltpu.make_async_copy(masters[t].at[j // 4, j % 4], stage.at[slot], st_sem.at[slot])

    for j in range(DEPTH):
        load(0, j, j).start()
    own_out = pltpu.make_async_copy(wo_ref, wout.at[pl.ds(0, 4)], own_sem)
    own_out.start()

    partners = [(d, 0, k, 0) for d in (1, 2, 3) for k in (0, 1)]
    partners += [(0, d, k, 0) for d in (1, 2, 3) for k in (0, 1)]
    partners += [(0, 0, k, d) for d in (1, 2, 3) for k in (0, 1)]
    partners += [(0, 0, 1, 0)]
    barrier = pltpu.get_barrier_semaphore()
    for p in partners:
        pl.semaphore_signal(barrier, inc=1, device_id=dev(*p), device_id_type=MESH)
    pl.semaphore_wait(barrier, len(partners))

    drains = []

    def cast(t):
        def one(j):
            slot = j % DEPTH
            load(t, j, slot).wait()
            ws[t, j // 4, j % 4] = stage[slot].astype(BF)
            return slot

        def step_a(j, carry):
            load(t, j + DEPTH, one(j)).start()
            return carry

        def step_b(j, carry):
            slot = one(j)
            if t < 2:
                load(t + 1, j + DEPTH - 16, slot).start()
            return carry

        lax.fori_loop(0, 16 - DEPTH, step_a, 0)
        lax.fori_loop(16 - DEPTH, 16, step_b, 0)

    def leg_one(t):
        group = []
        for d in (1, 3, 2, 0):
            for dc in (0, 1):
                i = d * 2 + dc
                xd, yd, cd = (x + d) % 4, (y + d) % 4, (c + dc) % 2
                src_a = ws.at[t, xd, :, cd, :, pl.ds(0, 384)]
                src_b = ws.at[t, :, yd, cd, :, pl.ds(384, 384)]
                if i == 0:
                    cp_a = pltpu.make_async_copy(src_a, mid_a.at[t, x, c], w1_r.at[t, 0, i])
                    cp_b = pltpu.make_async_copy(src_b, mid_b.at[t, y, c], w1_r.at[t, 1, i])
                else:
                    cp_a = remote(
                        src_a, mid_a.at[t, x, c], w1_s.at[t, 0, i], w1_r.at[t, 0, i],
                        dev(dx=d, dc=dc),
                    )
                    cp_b = remote(
                        src_b, mid_b.at[t, y, c], w1_s.at[t, 1, i], w1_r.at[t, 1, i],
                        dev(dy=d, dc=dc),
                    )
                    drains.extend([cp_a, cp_b])
                cp_a.start()
                cp_b.start()
                group += [(i, cp_a), (i, cp_b)]
        return group

    def wait_group(group):
        for i, cp in group:
            if i == 0:
                cp.wait()
            else:
                cp.wait_recv()

    def second(t, k):
        group = []
        for d in (1, 3, 2, 0):
            xd, yd = (x + d) % 4, (y + d) % 4
            if k is None:
                src_a, src_b = mid_a.at[t, :, :, yd], mid_b.at[t, :, :, xd]
                dst_a = wgu.at[t, :, y, :, :, pl.ds(0, 384)]
                dst_b = wgu.at[t, x, :, :, :, pl.ds(384, 384)]
                snd, rcv = w2_s.at[t], w2_r.at[t]
            else:
                src_a = mid_a.at[t, :, :, yd, pl.ds(16 * k, 16)]
                src_b = mid_b.at[t, :, :, xd, pl.ds(16 * k, 16)]
                dst_a = wd.at[k, :, y, :, :, pl.ds(0, 384)]
                dst_b = wd.at[k, x, :, :, :, pl.ds(384, 384)]
                snd, rcv = d2_s.at[k], d2_r.at[k]
            if d == 0:
                cp_a = pltpu.make_async_copy(src_a, dst_a, rcv.at[0, 0])
                cp_b = pltpu.make_async_copy(src_b, dst_b, rcv.at[1, 0])
            else:
                cp_a = remote(src_a, dst_a, snd.at[0, d], rcv.at[0, d], dev(dy=d))
                cp_b = remote(src_b, dst_b, snd.at[1, d], rcv.at[1, d], dev(dx=d))
                drains.extend([cp_a, cp_b])
            cp_a.start()
            cp_b.start()
            group += [(d, cp_a), (d, cp_b)]
        return group

    cast(0)
    first = [leg_one(0)]
    cast(1)
    first.append(leg_one(1))

    inv = 1.0 / math.sqrt(128.0)
    neg = -jnp.inf
    lane = lax.broadcasted_iota(jnp.int32, (32, 128), 1)
    for g in range(2):
        for h in range(8):
            for t in range(4):
                head = g * 8 + h
                o_s[:, g, t * 8 + h, :] = q_ref[t, :, head * 128:(head + 1) * 128].astype(F32)
    for s in range(8):
        if s < 4:
            nk_s[:, s, :] = nk_ref[s].astype(F32)
            nv_s[:, s, :] = nv_ref[s].astype(F32)
        else:
            nk_s[:, s, :] = jnp.zeros((16, 256), F32)
            nv_s[:, s, :] = jnp.zeros((16, 256), F32)
    fresh_ok = lax.broadcasted_iota(jnp.int32, (32, 8), 1) <= (
        lax.broadcasted_iota(jnp.int32, (32, 8), 0) >> 3
    )

    def attend(r, carry):
        ok = lane < len_ref[r]
        for g in range(2):
            cols = slice(g * 128, (g + 1) * 128)
            qq = o_s[r, g].astype(BF)
            s = jnp.where(ok, dot_nt(qq, ck_ref[r, :, cols]) * inv, neg)
            f = jnp.where(fresh_ok, dot_nt(qq, nk_s[r, :, cols].astype(BF)) * inv, neg)
            top = jnp.maximum(
                jnp.max(s, axis=-1, keepdims=True), jnp.max(f, axis=-1, keepdims=True)
            )
            es, ef = jnp.exp(s - top), jnp.exp(f - top)
            total = jnp.sum(es, axis=-1, keepdims=True) + jnp.sum(ef, axis=-1, keepdims=True)
            ps, pf = (es / total).astype(BF), (ef / total).astype(BF)
            o_s[r, g] = dot(ps, cv_ref[r, :, cols]) + dot(pf, nv_s[r, :, cols].astype(BF))
        return carry

    def attend_some(i, carry):
        for j in range(UNROLL):
            attend(i * UNROLL + j, 0)
        return carry

    lax.fori_loop(0, 16 // UNROLL, attend_some, 0)
    for g in range(2):
        for h in range(8):
            for t in range(4):
                head = g * 8 + h
                att[t * 16:(t + 1) * 16, head * 128:(head + 1) * 128] = o_s[
                    :, g, t * 8 + h, :
                ].astype(BF)

    toward = []
    for dz in (1, 3, 2):
        to = (z + dz) % 4
        cols = pl.ds(pl.multiple_of(to * 512, 512), 512)
        cp = remote(att.at[:, cols], attr.at[z], o_snd.at[dz - 1], o_rcv.at[dz - 1], dev(dz=dz))
        cp.start()
        toward.append(cp)
    mine = pltpu.make_async_copy(
        att.at[:, pl.ds(pl.multiple_of(z * 512, 512), 512)], attr.at[z], one_sem
    )
    mine.start()
    mine.wait()
    own_out.wait()
    for cp in toward:
        cp.wait()

    def project(n, carry):
        cols = pl.ds(pl.multiple_of(n * 512, 512), 512)
        got = dot(attr[...].reshape(256, 512), wout[0:4, :, :, cols].reshape(512, 512))
        ssend[0:4, 0, :, cols] = got.astype(BF).reshape(4, 64, 512)
        return carry

    lax.fori_loop(0, 4, project, 0)
    partial = []
    for dz in (1, 3, 2):
        cp = remote(
            ssend.at[(z + dz) % 4, 0], rs2.at[dz - 1], f_snd.at[dz - 1], f_rcv.at[dz - 1],
            dev(dz=dz),
        )
        cp.start()
        partial.append(cp)

    def project_own(n, carry):
        cols = pl.ds(pl.multiple_of(n * 512, 512), 512)
        got = dot(attr[z], wout[0:4, :, :, cols].reshape(512, 512))
        resid[:, cols] = x_ref[:, cols].astype(F32) + got
        return carry

    lax.fori_loop(0, 4, project_own, 0)
    cast(2)
    for cp in partial:
        cp.wait()
    for n in range(4):
        cols = slice(n * 512, (n + 1) * 512)
        total = resid[:, cols]
        for d in range(3):
            total = total + rs2[d, :, cols].astype(F32)
        resid[:, cols] = total
    res = resid[...]
    mean_square = jnp.mean(res * res, axis=-1, keepdims=True)
    normed = (res * lax.rsqrt(mean_square + 1e-06) * gain_ref[...].astype(F32).reshape(1, 2048)).astype(BF)
    ag_a[y, x, :, 0:1024] = normed[:, 0:1024]
    ag_b[x, y] = normed[:, 1024:2048]
    logits = dot(normed, router_ref[...])
    expert_i = lax.broadcasted_iota(jnp.int32, (128, 16), 0)
    eye_r = lax.broadcasted_iota(jnp.int32, (64, 16), 0)
    eye_c = lax.broadcasted_iota(jnp.int32, (64, 16), 1)
    member = jnp.zeros((64, 128), F32)
    for t in range(4):
        named = jnp.zeros((128, 16), F32)
        for k in range(8):
            named = named + (ids_ref[t, k:k + 1, :] == expert_i).astype(F32)
        eye = (eye_r == eye_c + t * 16).astype(F32).astype(BF)
        member = member + dot_nt(eye, named.astype(BF))
    row_i = lax.broadcasted_iota(jnp.int32, (64, 64), 0)
    col_i = lax.broadcasted_iota(jnp.int32, (64, 64), 1)
    before = ((row_i >> 4) == (col_i >> 4)) & (col_i < row_i)
    rank = dot(before.astype(F32).astype(BF), member.astype(BF))
    chosen = jnp.where(member > 0.5, logits, neg)
    chosen_exp = jnp.exp(chosen - jnp.max(chosen, axis=-1, keepdims=True))
    gates = chosen_exp / jnp.sum(chosen_exp, axis=-1, keepdims=True)
    ag_a[y, x, :, 1024:1152] = jnp.where(rank < 0.5, gates, -gates).astype(BF)

    ag1 = []
    for t in range(4):
        rows = pl.ds(t * 16, 16)
        group = []
        for d in (1, 3, 2):
            part_a, part_b = ag_a.at[y, x, rows], ag_b.at[x, y, rows]
            cp_a = remote(part_a, part_a, ag_s.at[t, 0, d], ag_r.at[t, 0, d], dev(dx=d))
            cp_b = remote(part_b, part_b, ag_s.at[t, 1, d], ag_r.at[t, 1, d], dev(dy=d))
            cp_a.start()
            cp_b.start()
            group += [cp_a, cp_b]
        ag1.append(group)
    ag2 = []
    for t in range(4):
        rows = pl.ds(t * 16, 16)
        for cp in ag1[t]:
            cp.wait()
        group = []
        for d in (1, 3, 2):
            part_a, part_b = ag_a.at[y, :, rows], ag_b.at[x, :, rows]
            cp_a = remote(part_a, part_a, ag_s.at[t, 2, d], ag_r.at[t, 2, d], dev(dy=d))
            cp_b = remote(part_b, part_b, ag_s.at[t, 3, d], ag_r.at[t, 3, d], dev(dx=d))
            cp_a.start()
            cp_b.start()
            group += [cp_a, cp_b]
        ag2.append(group)

    e_row = lax.broadcasted_iota(jnp.int32, (8, 128), 0)
    e_lane = lax.broadcasted_iota(jnp.int32, (8, 128), 1)
    pick = (e_lane == (e_row >> 1) * 32 + (e_row & 1) + x * 8 + y * 2).astype(F32).astype(BF)
    slot_i = lax.broadcasted_iota(jnp.int32, (8, 32, 256), 1)
    row_of = lax.broadcasted_iota(jnp.int32, (8, 32, 256), 2)
    same = (row_of >> 4) == (slot_i >> 1)
    sign = jnp.where((slot_i & 1) == 0, 1.0, -1.0).astype(F32)

    def select(t):
        rows = slice(t * 16, t * 16 + 16)
        dst = slice((t % 2) * 32, (t % 2) * 32 + 32)
        aux = ag_a[:, :, rows, 1024:1152].reshape(256, 128)
        code = dot_nt(pick, aux)
        signed = jnp.where(same, code[:, None, :] * sign, 0.0)
        weight = jnp.maximum(signed, 0.0).reshape(256, 256)
        pg[t] = weight.astype(BF)
        place = (weight > 0.0).astype(F32).astype(BF)
        for n in range(2):
            cols = slice(n * 512, (n + 1) * 512)
            got = dot(place, ag_a[:, :, rows, cols].reshape(256, 512))
            ssend[:, t // 2, dst, cols] = got.astype(BF).reshape(8, 32, 512)
        for n in range(2):
            cols = slice(n * 512, (n + 1) * 512)
            part = jnp.concatenate(
                [ag_b[:, k, rows, cols].reshape(64, 512) for k in range(4)], axis=0
            )
            got = dot(place, part)
            ssend[:, t // 2, dst, n * 512 + 1024:n * 512 + 1536] = got.astype(BF).reshape(8, 32, 512)

    column_devs = [(dz, dc) for dz in (1, 3, 2, 0) for dc in (0, 1)]
    def send_slots(t):
        group = []
        for dz, dc in column_devs:
            i = dz * 2 + dc
            to = ((z + dz) % 4) * 2 + (c + dc) % 2
            rows = pl.ds((t % 2) * 32, 32)
            src, dst = ssend.at[to, t // 2, rows], srecv.at[me, t // 2, rows]
            if i == 0:
                cp = pltpu.make_async_copy(src, dst, z_r.at[t, i])
            else:
                cp = remote(src, dst, z_s.at[t, i], z_r.at[t, i], dev(dz=dz, dc=dc))
            cp.start()
            group.append(cp)
        return group

    dispatch = []
    for t in range(4):
        for cp in ag2[t]:
            cp.wait()
        if t == 1:
            wait_group(first[0])
            g2 = second(0, None)
        if t == 2:
            wait_group(first[1])
            u2 = second(1, None)
        select(t)
        dispatch.append(send_slots(t))

    wait_group(g2)
    first.append(leg_one(2))
    wait_group(u2)

    for t in range(4):
        for cp in dispatch[t]:
            cp.wait()

    def hide_loop(t, carry):
        half = pl.ds(pl.multiple_of((t % 2) * 32, 32), 32)
        rows = srecv[:, t // 2, half, :].reshape(256, 2048)
        gate = dot(rows, wgu[0].reshape(2048, 768))
        up = dot(rows, wgu[1].reshape(2048, 768))
        ag_b[t, :, :, 0:768] = (jax.nn.silu(gate) * up).astype(BF).reshape(4, 64, 768)
        return carry

    lax.fori_loop(0, 2, hide_loop, 0)
    wait_group(first[2])
    d2 = [second(2, k) for k in range(4)]
    lax.fori_loop(2, 4, hide_loop, 0)

    def down(k):
        cols = slice(k * 512, (k + 1) * 512)
        wait_group(d2[k])

        def tile(t, carry):
            half = pl.ds(pl.multiple_of((t % 2) * 32, 32), 32)
            hidden = ag_b[t, :, :, 0:768].reshape(256, 768)
            got = dot_nt(hidden, wd[k].reshape(512, 768))
            srecv[:, t // 2, half, cols] = got.astype(BF).reshape(8, 32, 512)
            return carry

        lax.fori_loop(0, 4, tile, 0)
        group = []
        for dz, dc in column_devs:
            i = dz * 2 + dc
            to = ((z + dz) % 4) * 2 + (c + dc) % 2
            dst = wout.at[me, :, :, pl.ds(k * 512, 512)]
            if i == 0:
                cp = pltpu.make_async_copy(
                    srecv.at[me, :, :, pl.ds(k * 512, 512)], dst, t_r.at[k, i]
                )
            else:
                cp = remote(
                    srecv.at[to, :, :, pl.ds(k * 512, 512)], dst, t_s.at[k, i], t_r.at[k, i],
                    dev(dz=dz, dc=dc),
                )
                drains.append(cp)
            cp.start()
            group.append((i, cp))
        return group

    def combine(k, group):
        wait_group(group)

        def tile(t, carry):
            rows = pl.ds(pl.multiple_of(t * 16, 16), 16)
            src = pl.ds(pl.multiple_of((t % 2) * 32, 32), 32)
            got = wout[0:8, t // 2, src, k * 512:(k + 1) * 512].reshape(256, 512)
            part = dot_tn(pg[t], got).astype(BF)
            wout[8:16, :, rows, k * 512:k * 512 + 256] = part[:, 0:256].reshape(8, 2, 16, 256)
            for yy in range(4):
                for xx in range(4):
                    b = (yy * 4 + xx) * 16
                    wout[8 + xx * 2 + yy // 2, yy % 2, rows, k * 512 + 256:(k + 1) * 512] = part[
                        b:b + 16, 256:512
                    ]
            return carry

        lax.fori_loop(0, 4, tile, 0)
        sums = []
        for d in (1, 3, 2):
            xd, yd = (x + d) % 4, (y + d) % 4
            cp_a = remote(
                wout.at[pl.ds(8 + yd * 2, 2), :, :, pl.ds(k * 512, 256)], rs1.at[k, 0, d - 1],
                r1_s.at[k, 0, d - 1], r1_r.at[k, 0, d - 1], dev(dy=d),
            )
            cp_b = remote(
                wout.at[pl.ds(8 + xd * 2, 2), :, :, pl.ds(k * 512 + 256, 256)],
                rs1.at[k, 1, d - 1],
                r1_s.at[k, 1, d - 1], r1_r.at[k, 1, d - 1], dev(dx=d),
            )
            cp_a.start()
            cp_b.start()
            sums += [cp_a, cp_b]
        drains.extend(sums)
        return sums

    def halfway(k, sums):
        for cp in sums:
            cp.wait_recv()
        for route in range(2):
            mine = (y, x)[route]
            lanes = slice(k * 512 + route * 256, k * 512 + route * 256 + 256)
            total = wout[pl.ds(8 + mine * 2, 2), :, :, lanes].reshape(256, 256).astype(F32)
            for d in range(3):
                total = total + rs1[k, route, d].reshape(256, 256).astype(F32)
            ag_a[k, :, :, route * 256:(route + 1) * 256] = total.astype(BF).reshape(4, 64, 256)
        group = []
        for d in (1, 3, 2):
            xd, yd = (x + d) % 4, (y + d) % 4
            cp_a = remote(
                ag_a.at[k, xd, :, pl.ds(0, 256)], rs2.at[d - 1, :, pl.ds(k * 512, 256)],
                r2_s.at[k, 0, d - 1], r2_r.at[k, 0, d - 1], dev(dx=d),
            )
            cp_b = remote(
                ag_a.at[k, yd, :, pl.ds(256, 256)],
                rs2.at[d - 1, :, pl.ds(k * 512 + 256, 256)],
                r2_s.at[k, 1, d - 1], r2_r.at[k, 1, d - 1], dev(dy=d),
            )
            cp_a.start()
            cp_b.start()
            group += [cp_a, cp_b]
        drains.extend(group)
        return group

    def close(k, group):
        for cp in group:
            cp.wait_recv()
        for route in range(2):
            mine = (x, y)[route]
            total = ag_a[k, mine, :, route * 256:(route + 1) * 256].astype(F32)
            for d in range(3):
                total = total + rs2[d, :, k * 512 + route * 256:k * 512 + (route + 1) * 256].astype(F32)
            for i in range(2):
                o_s[k * 4 + route * 2 + i] = total[:, i * 128:(i + 1) * 128].reshape(2, 32, 128)

    backs, sums, ends = {}, {}, {}
    for k in range(7):
        if k < 4:
            backs[k] = down(k)
        if 0 <= k - 1 < 4:
            sums[k - 1] = combine(k - 1, backs[k - 1])
        if 0 <= k - 2 < 4:
            ends[k - 2] = halfway(k - 2, sums[k - 2])
        if 0 <= k - 3 < 4:
            close(k - 3, ends[k - 3])

    p_i = lax.broadcasted_iota(jnp.int32, (512, 512), 0)
    o_i = lax.broadcasted_iota(jnp.int32, (512, 512), 1)
    perm = (o_i == ((p_i >> 4) & 7) * 64 + (p_i >> 7) * 16 + (p_i & 15)).astype(F32).astype(BF)
    for g in range(4):
        v = jnp.concatenate(
            [o_s[k * 4 + g].reshape(64, 128) for k in range(4)], axis=1
        )
        hi = v.astype(BF)
        lo = (v - hi.astype(F32)).astype(BF)
        out_ref[:, g * 512:(g + 1) * 512] = (
            resid[:, g * 512:(g + 1) * 512] + dot(hi, perm) + dot(lo, perm)
        )
    for cp in drains:
        cp.wait_send()


def per_device(
    inputs, cache_keys, cache_values, lengths, new_keys, new_values, queries, out_weight,
    norm_gain, router, experts, master_gate, master_up, master_down,
):
    vm = pl.BlockSpec(memory_space=pltpu.VMEM)
    anyspace = pl.BlockSpec(memory_space=pl.ANY)
    dma = pltpu.SemaphoreType.DMA
    shape5 = (4, 4, 2, 64, 768)
    out = pl.pallas_call(
        kernel,
        out_shape=jax.ShapeDtypeStruct((64, 2048), F32),
        in_specs=[vm] * 9 + [pl.BlockSpec(memory_space=pltpu.SMEM)] + [anyspace] * 4,
        out_specs=vm,
        scratch_shapes=[
            pltpu.VMEM((DEPTH, 2, 64, 768), F32),
            pltpu.VMEM((3, 4, 4, 2, 64, 768), BF),
            pltpu.VMEM((3, 4, 2, 4, 64, 384), BF),
            pltpu.VMEM((3, 4, 2, 4, 64, 384), BF),
            pltpu.VMEM((2, 4, 4, 2, 64, 768), BF),
            pltpu.VMEM((4, 4, 4, 2, 16, 768), BF),
            pltpu.VMEM((16, 2, 64, 2048), BF),
            pltpu.VMEM((4, 4, 64, 1152), BF),
            pltpu.VMEM((4, 4, 64, 1024), BF),
            pltpu.VMEM((8, 2, 64, 2048), BF),
            pltpu.VMEM((8, 2, 64, 2048), BF),
            pltpu.VMEM((16, 2, 32, 128), F32),
            pltpu.VMEM((16, 8, 256), F32),
            pltpu.VMEM((16, 8, 256), F32),
            pltpu.VMEM((64, 2048), BF),
            pltpu.VMEM((4, 64, 512), BF),
            pltpu.VMEM((64, 2048), F32),
            pltpu.VMEM((4, 256, 256), BF),
            pltpu.VMEM((4, 2, 3, 2, 2, 64, 256), BF),
            pltpu.VMEM((3, 64, 2048), BF),
            dma((DEPTH,)),
            dma((3, 2, 8)), dma((3, 2, 8)),
            dma((2, 2, 4)), dma((2, 2, 4)),
            dma((4, 2, 4)), dma((4, 2, 4)),
            dma, dma((3,)), dma((3,)), dma((3,)), dma((3,)), dma,
            dma((4, 4, 4)), dma((4, 4, 4)),
            dma((4, 8)), dma((4, 8)),
            dma((4, 8)), dma((4, 8)),
            dma((4, 2, 3)), dma((4, 2, 3)),
            dma((4, 2, 3)), dma((4, 2, 3)),
        ],
        compiler_params=pltpu.CompilerParams(
            collective_id=0, has_side_effects=True, vmem_limit_bytes=66_900_000
        ),
        name="moe_decode",
    )(
        inputs.reshape(64, 2048), queries, cache_keys, cache_values, new_keys, new_values,
        norm_gain, router, experts.transpose(0, 2, 1), lengths,
        out_weight.reshape(4, 2, 64, 2048),
        master_gate.reshape(shape5), master_up.reshape(shape5), master_down.reshape(shape5),
    )
    return out.astype(BF).reshape(4, 16, 2048)


def solution(mesh):
    return jax.shard_map(
        per_device,
        mesh=mesh,
        in_specs=(
            P(None, ("fsdp", "expert"), None),
            P(("fsdp", "expert"), None, None),
            P(("fsdp", "expert"), None, None),
            P(("fsdp", "expert")),
            P(None, ("fsdp", "expert"), None),
            P(None, ("fsdp", "expert"), None),
            P(None, ("fsdp", "expert"), None),
            P("fsdp", None),
            P(),
            P(),
            P(None, ("fsdp", "expert"), None),
            P("fsdp", "expert", None),
            P("fsdp", "expert", None),
            P("fsdp", "expert", None),
        ),
        out_specs=P(None, ("fsdp", "expert"), None),
        check_vma=False,
    )
```

```python
import functools
import math

import jax
import jax.numpy as jnp
from jax import lax
from jax.experimental import pallas as pl
from jax.experimental.pallas import tpu as pltpu
from jax.sharding import PartitionSpec as P

MESH = pl.DeviceIdType.MESH
BF = jnp.bfloat16
F32 = jnp.float32
NT = (((1,), (1,)), ((), ()))
TN = (((0,), (0,)), ((), ()))
DEPTH = 8
UNROLL = 4


def dot(a, b):
    return jnp.dot(a, b, preferred_element_type=F32)


def dot_nt(a, b):
    return lax.dot_general(a, b, NT, preferred_element_type=F32)


def dot_tn(a, b):
    return lax.dot_general(a, b, TN, preferred_element_type=F32)


def kernel(
    x_ref, q_ref, nk_ref, nv_ref, gain_ref, ids_ref, len_ref,
    ck_hbm, cv_hbm, router_hbm, wo_ref, mg_ref, mu_ref, md_ref,
    out_ref,
    ck_ref, cv_ref, router_ref, stage, ws, mid_a, mid_b, wgu, wd, wout, ag_a, ag_b, ssend, srecv,
    o_s, nk_s, nv_s, att, attr, resid, pg, rs1, rs2,
    st_sem, in_sem, w1_s, w1_r, d1_s, d1_r, w2_s, w2_r, d2_s, d2_r, own_sem, o_snd, o_rcv, f_snd, f_rcv, one_sem,
    ag_s, ag_r, z_s, z_r, t_s, t_r, r1_s, r1_r, r2_s, r2_r,
):
    z = lax.axis_index("fsdp")
    e = lax.axis_index("expert")
    x = e // 8
    y = (e // 2) % 4
    c = e % 2
    me = z * 2 + c

    def dev(dx=0, dy=0, dc=0, dz=0):
        return (
            (z + dz) % 4,
            ((x + dx) % 4) * 8 + ((y + dy) % 4) * 2 + (c + dc) % 2,
        )

    def remote(src, dst, snd, rcv, target):
        return pltpu.make_async_remote_copy(
            src_ref=src, dst_ref=dst, send_sem=snd, recv_sem=rcv,
            device_id=target, device_id_type=MESH,
        )

    masters = (mg_ref, mu_ref, md_ref)

    def load(t, j, slot):
        return pltpu.make_async_copy(masters[t].at[j // 4, j % 4], stage.at[slot], st_sem.at[slot])

    for j in range(DEPTH):
        load(0, j, j).start()
    own_out = pltpu.make_async_copy(wo_ref, wout.at[pl.ds(0, 4)], own_sem)
    own_out.start()
    local_ins = [
        pltpu.make_async_copy(src, dst, in_sem.at[i])
        for i, (src, dst) in enumerate(
            ((ck_hbm, ck_ref), (cv_hbm, cv_ref), (router_hbm, router_ref))
        )
    ]
    for cp in local_ins:
        cp.start()

    partners = [(d, 0, k, 0) for d in (1, 2, 3) for k in (0, 1)]
    partners += [(0, d, k, 0) for d in (1, 2, 3) for k in (0, 1)]
    partners += [(0, 0, k, d) for d in (1, 2, 3) for k in (0, 1)]
    partners += [(0, 0, 1, 0)]
    barrier = pltpu.get_barrier_semaphore()
    for p in partners:
        pl.semaphore_signal(barrier, inc=1, device_id=dev(*p), device_id_type=MESH)
    pl.semaphore_wait(barrier, len(partners))

    drains = []

    def cast(t):
        def one(j):
            slot = j % DEPTH
            load(t, j, slot).wait()
            ws[t, j // 4, j % 4] = stage[slot].astype(BF)
            return slot

        def step_a(j, carry):
            load(t, j + DEPTH, one(j)).start()
            return carry

        def step_b(j, carry):
            slot = one(j)
            if t < 2:
                load(t + 1, j + DEPTH - 16, slot).start()
            return carry

        lax.fori_loop(0, 16 - DEPTH, step_a, 0)
        lax.fori_loop(16 - DEPTH, 16, step_b, 0)

    def leg_one(t, k=None):
        group = []
        snd, rcv = (w1_s.at[t], w1_r.at[t]) if k is None else (d1_s.at[k], d1_r.at[k])
        rows = pl.ds(0, 64) if k is None else pl.ds(k * 16, 16)
        for d in (1, 3, 2, 0):
            for dc in (0, 1):
                i = d * 2 + dc
                xd, yd, cd = (x + d) % 4, (y + d) % 4, (c + dc) % 2
                src_a = ws.at[t, xd, :, cd, rows, pl.ds(0, 384)]
                src_b = ws.at[t, :, yd, cd, rows, pl.ds(384, 384)]
                dst_a, dst_b = mid_a.at[t, x, c, :, rows], mid_b.at[t, y, c, :, rows]
                if i == 0:
                    cp_a = pltpu.make_async_copy(src_a, dst_a, rcv.at[0, i])
                    cp_b = pltpu.make_async_copy(src_b, dst_b, rcv.at[1, i])
                else:
                    cp_a = remote(
                        src_a, dst_a, snd.at[0, i], rcv.at[0, i], dev(dx=d, dc=dc)
                    )
                    cp_b = remote(
                        src_b, dst_b, snd.at[1, i], rcv.at[1, i], dev(dy=d, dc=dc)
                    )
                    drains.extend([cp_a, cp_b])
                cp_a.start()
                cp_b.start()
                group += [(i, cp_a), (i, cp_b)]
        return group

    def wait_group(group):
        for i, cp in group:
            if i == 0:
                cp.wait()
            else:
                cp.wait_recv()

    def second(t, k):
        group = []
        for d in (1, 3, 2, 0):
            xd, yd = (x + d) % 4, (y + d) % 4
            if k is None:
                src_a, src_b = mid_a.at[t, :, :, yd], mid_b.at[t, :, :, xd]
                dst_a = wgu.at[t, :, y, :, :, pl.ds(0, 384)]
                dst_b = wgu.at[t, x, :, :, :, pl.ds(384, 384)]
                snd, rcv = w2_s.at[t], w2_r.at[t]
            else:
                src_a = mid_a.at[t, :, :, yd, pl.ds(16 * k, 16)]
                src_b = mid_b.at[t, :, :, xd, pl.ds(16 * k, 16)]
                dst_a = wd.at[k, :, y, :, :, pl.ds(0, 384)]
                dst_b = wd.at[k, x, :, :, :, pl.ds(384, 384)]
                snd, rcv = d2_s.at[k], d2_r.at[k]
            if d == 0:
                cp_a = pltpu.make_async_copy(src_a, dst_a, rcv.at[0, 0])
                cp_b = pltpu.make_async_copy(src_b, dst_b, rcv.at[1, 0])
            else:
                cp_a = remote(src_a, dst_a, snd.at[0, d], rcv.at[0, d], dev(dy=d))
                cp_b = remote(src_b, dst_b, snd.at[1, d], rcv.at[1, d], dev(dx=d))
                drains.extend([cp_a, cp_b])
            cp_a.start()
            cp_b.start()
            group += [(d, cp_a), (d, cp_b)]
        return group

    cast(0)
    first = [leg_one(0)]
    for cp in local_ins:
        cp.wait()

    inv = 1.0 / math.sqrt(128.0)
    neg = -jnp.inf
    lane = lax.broadcasted_iota(jnp.int32, (32, 136), 1)
    fresh_ok = (lane >= 128) & (
        lane - 128 <= (lax.broadcasted_iota(jnp.int32, (32, 136), 0) >> 3)
    )
    for g in range(2):
        for h in range(8):
            for t in range(4):
                head = g * 8 + h
                o_s[:, g, t * 8 + h, :] = q_ref[t, :, head * 128:(head + 1) * 128].astype(F32)
    for s in range(8):
        if s < 4:
            nk_s[:, s, :] = nk_ref[s].astype(F32)
            nv_s[:, s, :] = nv_ref[s].astype(F32)
        else:
            nk_s[:, s, :] = jnp.zeros((16, 256), F32)
            nv_s[:, s, :] = jnp.zeros((16, 256), F32)
    def attend(r, carry):
        ok = fresh_ok | (lane < len_ref[r])
        for g in range(2):
            cols = slice(g * 128, (g + 1) * 128)
            qq = o_s[r, g].astype(BF)
            keys = jnp.concatenate([ck_ref[r, :, cols], nk_s[r, :, cols].astype(BF)], axis=0)
            values = jnp.concatenate([cv_ref[r, :, cols], nv_s[r, :, cols].astype(BF)], axis=0)
            s = jnp.where(ok, dot_nt(qq, keys) * inv, neg)
            es = jnp.exp(s - jnp.max(s, axis=-1, keepdims=True))
            ps = (es / jnp.sum(es, axis=-1, keepdims=True)).astype(BF)
            o_s[r, g] = dot(ps, values)
        return carry

    def attend_some(i, carry):
        for j in range(UNROLL):
            attend(i * UNROLL + j, 0)
        return carry

    lax.fori_loop(0, 16 // UNROLL, attend_some, 0)
    for g in range(2):
        for h in range(8):
            for t in range(4):
                head = g * 8 + h
                att[t * 16:(t + 1) * 16, head * 128:(head + 1) * 128] = o_s[
                    :, g, t * 8 + h, :
                ].astype(BF)

    toward = []
    for dz in (1, 3, 2):
        to = (z + dz) % 4
        cols = pl.ds(pl.multiple_of(to * 512, 512), 512)
        cp = remote(att.at[:, cols], attr.at[z], o_snd.at[dz - 1], o_rcv.at[dz - 1], dev(dz=dz))
        cp.start()
        toward.append(cp)
    mine = pltpu.make_async_copy(
        att.at[:, pl.ds(pl.multiple_of(z * 512, 512), 512)], attr.at[z], one_sem
    )
    mine.start()
    cast(1)
    first.append(leg_one(1))
    mine.wait()
    own_out.wait()
    for cp in toward:
        cp.wait()

    def project(n, carry):
        cols = pl.ds(pl.multiple_of(n * 512, 512), 512)
        got = dot(attr[...].reshape(256, 512), wout[0:4, :, :, cols].reshape(512, 512))
        ssend[0:4, 0, :, cols] = got.astype(BF).reshape(4, 64, 512)
        return carry

    lax.fori_loop(0, 4, project, 0)
    partial = []
    for dz in (1, 3, 2):
        cp = remote(
            ssend.at[(z + dz) % 4, 0], rs2.at[dz - 1], f_snd.at[dz - 1], f_rcv.at[dz - 1],
            dev(dz=dz),
        )
        cp.start()
        partial.append(cp)

    def project_own(n, carry):
        cols = pl.ds(pl.multiple_of(n * 512, 512), 512)
        got = dot(attr[z], wout[0:4, :, :, cols].reshape(512, 512))
        resid[:, cols] = x_ref[:, cols].astype(F32) + got
        return carry

    lax.fori_loop(0, 4, project_own, 0)
    cast(2)
    for cp in partial:
        cp.wait()
    for n in range(4):
        cols = slice(n * 512, (n + 1) * 512)
        total = resid[:, cols]
        for d in range(3):
            total = total + rs2[d, :, cols].astype(F32)
        resid[:, cols] = total
    res = resid[...]
    mean_square = jnp.mean(res * res, axis=-1, keepdims=True)
    normed = (res * lax.rsqrt(mean_square + 1e-06) * gain_ref[...].astype(F32).reshape(1, 2048)).astype(BF)
    ag_a[y, x, :, 0:1024] = normed[:, 0:1024]
    ag_b[x, y] = normed[:, 1024:2048]
    logits = dot(normed, router_ref[...])
    expert_i = lax.broadcasted_iota(jnp.int32, (128, 16), 0)
    eye_r = lax.broadcasted_iota(jnp.int32, (64, 16), 0)
    eye_c = lax.broadcasted_iota(jnp.int32, (64, 16), 1)
    member = jnp.zeros((64, 128), F32)
    for t in range(4):
        named = jnp.zeros((128, 16), F32)
        for k in range(8):
            named = named + (ids_ref[t, k:k + 1, :] == expert_i).astype(F32)
        eye = (eye_r == eye_c + t * 16).astype(F32).astype(BF)
        member = member + dot_nt(eye, named.astype(BF))
    row_i = lax.broadcasted_iota(jnp.int32, (64, 64), 0)
    col_i = lax.broadcasted_iota(jnp.int32, (64, 64), 1)
    before = ((row_i >> 4) == (col_i >> 4)) & (col_i < row_i)
    rank = dot(before.astype(F32).astype(BF), member.astype(BF))
    chosen = jnp.where(member > 0.5, logits, neg)
    chosen_exp = jnp.exp(chosen - jnp.max(chosen, axis=-1, keepdims=True))
    gates = chosen_exp / jnp.sum(chosen_exp, axis=-1, keepdims=True)
    ag_a[y, x, :, 1024:1152] = jnp.where(rank < 0.5, gates, -gates).astype(BF)

    ag1 = []
    for t in range(4):
        rows = pl.ds(t * 16, 16)
        group = []
        for d in (1, 3, 2):
            part_a, part_b = ag_a.at[y, x, rows], ag_b.at[x, y, rows]
            cp_a = remote(part_a, part_a, ag_s.at[t, 0, d], ag_r.at[t, 0, d], dev(dx=d))
            cp_b = remote(part_b, part_b, ag_s.at[t, 1, d], ag_r.at[t, 1, d], dev(dy=d))
            cp_a.start()
            cp_b.start()
            group += [cp_a, cp_b]
        ag1.append(group)
    ag2, ag3 = [], []

    def gather_two(t):
        rows = pl.ds(t * 16, 16)
        for cp in ag1[t]:
            cp.wait()
        group = []
        for d in (1, 3):
            part_a, part_b = ag_a.at[y, :, rows], ag_b.at[x, :, rows]
            cp_a = remote(part_a, part_a, ag_s.at[t, 2, d], ag_r.at[t, 2, d], dev(dy=d))
            cp_b = remote(part_b, part_b, ag_s.at[t, 3, d], ag_r.at[t, 3, d], dev(dx=d))
            cp_a.start()
            cp_b.start()
            group += [cp_a, cp_b]
        ag2.append(group)

    def gather_three(t):
        rows = pl.ds(t * 16, 16)
        for cp in ag2[t]:
            cp.wait()
        group = []
        for i, d in ((0, 1), (2, 3)):
            half = pl.ds(i, 2)
            part_a = ag_a.at[(y + 4 - d) % 4, half, rows]
            part_b = ag_b.at[(x + 4 - d) % 4, half, rows]
            cp_a = remote(part_a, part_a, ag_s.at[t, 2, i], ag_r.at[t, 2, i], dev(dy=d))
            cp_b = remote(part_b, part_b, ag_s.at[t, 3, i], ag_r.at[t, 3, i], dev(dx=d))
            cp_a.start()
            cp_b.start()
            group += [cp_a, cp_b]
        ag3.append(group)

    e_row = lax.broadcasted_iota(jnp.int32, (8, 128), 0)
    e_lane = lax.broadcasted_iota(jnp.int32, (8, 128), 1)
    pick = (e_lane == (e_row >> 1) * 32 + (e_row & 1) + x * 8 + y * 2).astype(F32).astype(BF)
    slot_i = lax.broadcasted_iota(jnp.int32, (8, 32, 256), 1)
    row_of = lax.broadcasted_iota(jnp.int32, (8, 32, 256), 2)
    same = (row_of >> 4) == (slot_i >> 1)
    sign = jnp.where((slot_i & 1) == 0, 1.0, -1.0).astype(F32)

    def select(t):
        rows = slice(t * 16, t * 16 + 16)
        dst = slice((t % 2) * 32, (t % 2) * 32 + 32)
        aux = ag_a[:, :, rows, 1024:1152].reshape(256, 128)
        code = dot_nt(pick, aux)
        signed = jnp.where(same, code[:, None, :] * sign, 0.0)
        weight = jnp.maximum(signed, 0.0).reshape(256, 256)
        pg[t] = weight.astype(BF)
        place = (weight > 0.0).astype(F32).astype(BF)
        for n in range(2):
            cols = slice(n * 512, (n + 1) * 512)
            got = dot(place, ag_a[:, :, rows, cols].reshape(256, 512))
            ssend[:, t // 2, dst, cols] = got.astype(BF).reshape(8, 32, 512)
        for n in range(2):
            cols = slice(n * 512, (n + 1) * 512)
            part = jnp.concatenate(
                [ag_b[:, k, rows, cols].reshape(64, 512) for k in range(4)], axis=0
            )
            got = dot(place, part)
            ssend[:, t // 2, dst, n * 512 + 1024:n * 512 + 1536] = got.astype(BF).reshape(8, 32, 512)

    column_devs = [(dz, dc) for dz in (1, 3, 2, 0) for dc in (0, 1)]
    def send_slots(t):
        group = []
        for dz, dc in column_devs:
            i = dz * 2 + dc
            to = ((z + dz) % 4) * 2 + (c + dc) % 2
            rows = pl.ds((t % 2) * 32, 32)
            src, dst = ssend.at[to, t // 2, rows], srecv.at[me, t // 2, rows]
            if i == 0:
                cp = pltpu.make_async_copy(src, dst, z_r.at[t, i])
            else:
                cp = remote(src, dst, z_s.at[t, i], z_r.at[t, i], dev(dz=dz, dc=dc))
            cp.start()
            group.append(cp)
        return group

    dispatch = []
    for step in range(6):
        if step < 4:
            gather_two(step)
        if 1 <= step < 5:
            gather_three(step - 1)
        if step == 4:
            wait_group(first[0])
            g2 = second(0, None)
        if step >= 2:
            t = step - 2
            for cp in ag3[t]:
                cp.wait()
            if t == 2:
                wait_group(first[1])
                u2 = second(1, None)
            select(t)
            dispatch.append(send_slots(t))

    d1 = [leg_one(2, 0)]
    wait_group(g2)
    d1.append(leg_one(2, 1))
    wait_group(d1[0])
    d2 = [second(2, 0)]
    wait_group(u2)
    d1.append(leg_one(2, 2))

    for t in range(4):
        for cp in dispatch[t]:
            cp.wait()

    def hide_loop(t, carry):
        half = pl.ds(pl.multiple_of((t % 2) * 32, 32), 32)
        rows = srecv[:, t // 2, half, :].reshape(256, 2048)
        gate = dot(rows, wgu[0].reshape(2048, 768))
        up = dot(rows, wgu[1].reshape(2048, 768))
        ag_b[t, :, :, 0:768] = (jax.nn.silu(gate) * up).astype(BF).reshape(4, 64, 768)
        return carry

    lax.fori_loop(0, 2, hide_loop, 0)
    wait_group(d1[1])
    d2.append(second(2, 1))
    d1.append(leg_one(2, 3))
    lax.fori_loop(2, 4, hide_loop, 0)

    def down(k):
        cols = slice(k * 512, (k + 1) * 512)
        wait_group(d2[k])

        def tile(t, carry):
            half = pl.ds(pl.multiple_of((t % 2) * 32, 32), 32)
            hidden = ag_b[t, :, :, 0:768].reshape(256, 768)
            got = dot_nt(hidden, wd[k].reshape(512, 768))
            srecv[:, t // 2, half, cols] = got.astype(BF).reshape(8, 32, 512)
            return carry

        lax.fori_loop(0, 4, tile, 0)
        group = []
        for dz, dc in column_devs:
            i = dz * 2 + dc
            to = ((z + dz) % 4) * 2 + (c + dc) % 2
            dst = wout.at[me, :, :, pl.ds(k * 512, 512)]
            if i == 0:
                cp = pltpu.make_async_copy(
                    srecv.at[me, :, :, pl.ds(k * 512, 512)], dst, t_r.at[k, i]
                )
            else:
                cp = remote(
                    srecv.at[to, :, :, pl.ds(k * 512, 512)], dst, t_s.at[k, i], t_r.at[k, i],
                    dev(dz=dz, dc=dc),
                )
                drains.append(cp)
            cp.start()
            group.append((i, cp))
        return group

    def combine(k, group):
        wait_group(group)

        def tile(t, carry):
            rows = pl.ds(pl.multiple_of(t * 16, 16), 16)
            src = pl.ds(pl.multiple_of((t % 2) * 32, 32), 32)
            got = wout[0:8, t // 2, src, k * 512:(k + 1) * 512].reshape(256, 512)
            part = dot_tn(pg[t], got).astype(BF)
            wout[8:16, :, rows, k * 512:k * 512 + 256] = part[:, 0:256].reshape(8, 2, 16, 256)
            for yy in range(4):
                for xx in range(4):
                    b = (yy * 4 + xx) * 16
                    wout[8 + xx * 2 + yy // 2, yy % 2, rows, k * 512 + 256:(k + 1) * 512] = part[
                        b:b + 16, 256:512
                    ]
            return carry

        lax.fori_loop(0, 4, tile, 0)
        sums = []
        for d in (1, 3, 2):
            xd, yd = (x + d) % 4, (y + d) % 4
            cp_a = remote(
                wout.at[pl.ds(8 + yd * 2, 2), :, :, pl.ds(k * 512, 256)], rs1.at[k, 0, d - 1],
                r1_s.at[k, 0, d - 1], r1_r.at[k, 0, d - 1], dev(dy=d),
            )
            cp_b = remote(
                wout.at[pl.ds(8 + xd * 2, 2), :, :, pl.ds(k * 512 + 256, 256)],
                rs1.at[k, 1, d - 1],
                r1_s.at[k, 1, d - 1], r1_r.at[k, 1, d - 1], dev(dx=d),
            )
            cp_a.start()
            cp_b.start()
            sums += [cp_a, cp_b]
        drains.extend(sums)
        return sums

    def halfway(k, sums):
        for cp in sums:
            cp.wait_recv()
        for route in range(2):
            mine = (y, x)[route]
            lanes = slice(k * 512 + route * 256, k * 512 + route * 256 + 256)
            total = wout[pl.ds(8 + mine * 2, 2), :, :, lanes].reshape(256, 256).astype(F32)
            for d in range(3):
                total = total + rs1[k, route, d].reshape(256, 256).astype(F32)
            ag_a[k, :, :, route * 256:(route + 1) * 256] = total.astype(BF).reshape(4, 64, 256)
        group = []
        for d in (1, 3, 2):
            xd, yd = (x + d) % 4, (y + d) % 4
            cp_a = remote(
                ag_a.at[k, xd, :, pl.ds(0, 256)], rs2.at[d - 1, :, pl.ds(k * 512, 256)],
                r2_s.at[k, 0, d - 1], r2_r.at[k, 0, d - 1], dev(dx=d),
            )
            cp_b = remote(
                ag_a.at[k, yd, :, pl.ds(256, 256)],
                rs2.at[d - 1, :, pl.ds(k * 512 + 256, 256)],
                r2_s.at[k, 1, d - 1], r2_r.at[k, 1, d - 1], dev(dy=d),
            )
            cp_a.start()
            cp_b.start()
            group += [cp_a, cp_b]
        drains.extend(group)
        return group

    def close(k, group):
        for cp in group:
            cp.wait_recv()
        for route in range(2):
            mine = (x, y)[route]
            total = ag_a[k, mine, :, route * 256:(route + 1) * 256].astype(F32)
            for d in range(3):
                total = total + rs2[d, :, k * 512 + route * 256:k * 512 + (route + 1) * 256].astype(F32)
            for i in range(2):
                o_s[k * 4 + route * 2 + i] = total[:, i * 128:(i + 1) * 128].reshape(2, 32, 128)

    backs, sums, ends = {}, {}, {}
    for k in range(7):
        if k < 4:
            backs[k] = down(k)
        if k < 2:
            wait_group(d1[k + 2])
            d2.append(second(2, k + 2))
        if 0 <= k - 1 < 4:
            sums[k - 1] = combine(k - 1, backs[k - 1])
        if 0 <= k - 2 < 4:
            ends[k - 2] = halfway(k - 2, sums[k - 2])
        if 0 <= k - 3 < 4:
            close(k - 3, ends[k - 3])

    p_i = lax.broadcasted_iota(jnp.int32, (512, 512), 0)
    o_i = lax.broadcasted_iota(jnp.int32, (512, 512), 1)
    perm = (o_i == ((p_i >> 4) & 7) * 64 + (p_i >> 7) * 16 + (p_i & 15)).astype(F32).astype(BF)
    for g in range(4):
        v = jnp.concatenate(
            [o_s[k * 4 + g].reshape(64, 128) for k in range(4)], axis=1
        )
        hi = v.astype(BF)
        lo = (v - hi.astype(F32)).astype(BF)
        out_ref[:, g * 512:(g + 1) * 512] = (
            resid[:, g * 512:(g + 1) * 512] + dot(hi, perm) + dot(lo, perm)
        )
    for cp in drains:
        cp.wait_send()


def per_device(
    inputs, cache_keys, cache_values, lengths, new_keys, new_values, queries, out_weight,
    norm_gain, router, experts, master_gate, master_up, master_down,
):
    vm = pl.BlockSpec(memory_space=pltpu.VMEM)
    anyspace = pl.BlockSpec(memory_space=pl.ANY)
    dma = pltpu.SemaphoreType.DMA
    shape5 = (4, 4, 2, 64, 768)
    out = pl.pallas_call(
        kernel,
        out_shape=jax.ShapeDtypeStruct((64, 2048), F32),
        in_specs=[vm] * 6 + [pl.BlockSpec(memory_space=pltpu.SMEM)] + [anyspace] * 7,
        out_specs=vm,
        scratch_shapes=[
            pltpu.VMEM((16, 128, 256), BF),
            pltpu.VMEM((16, 128, 256), BF),
            pltpu.VMEM((2048, 128), BF),
            pltpu.VMEM((DEPTH, 2, 64, 768), F32),
            pltpu.VMEM((3, 4, 4, 2, 64, 768), BF),
            pltpu.VMEM((3, 4, 2, 4, 64, 384), BF),
            pltpu.VMEM((3, 4, 2, 4, 64, 384), BF),
            pltpu.VMEM((2, 4, 4, 2, 64, 768), BF),
            pltpu.VMEM((4, 4, 4, 2, 16, 768), BF),
            pltpu.VMEM((16, 2, 64, 2048), BF),
            pltpu.VMEM((4, 4, 64, 1152), BF),
            pltpu.VMEM((4, 4, 64, 1024), BF),
            pltpu.VMEM((8, 2, 64, 2048), BF),
            pltpu.VMEM((8, 2, 64, 2048), BF),
            pltpu.VMEM((16, 2, 32, 128), F32),
            pltpu.VMEM((16, 8, 256), F32),
            pltpu.VMEM((16, 8, 256), F32),
            pltpu.VMEM((64, 2048), BF),
            pltpu.VMEM((4, 64, 512), BF),
            pltpu.VMEM((64, 2048), F32),
            pltpu.VMEM((4, 256, 256), BF),
            pltpu.VMEM((4, 2, 3, 2, 2, 64, 256), BF),
            pltpu.VMEM((3, 64, 2048), BF),
            dma((DEPTH,)),
            dma((3,)), dma((2, 2, 8)), dma((2, 2, 8)), dma((4, 2, 8)), dma((4, 2, 8)),
            dma((2, 2, 4)), dma((2, 2, 4)),
            dma((4, 2, 4)), dma((4, 2, 4)),
            dma, dma((3,)), dma((3,)), dma((3,)), dma((3,)), dma,
            dma((4, 4, 4)), dma((4, 4, 4)),
            dma((4, 8)), dma((4, 8)),
            dma((4, 8)), dma((4, 8)),
            dma((4, 2, 3)), dma((4, 2, 3)),
            dma((4, 2, 3)), dma((4, 2, 3)),
        ],
        compiler_params=pltpu.CompilerParams(
            collective_id=0, has_side_effects=True, vmem_limit_bytes=66_900_000
        ),
        name="moe_decode",
    )(
        inputs.reshape(64, 2048), queries, new_keys, new_values,
        norm_gain, experts.transpose(0, 2, 1), lengths, cache_keys, cache_values, router,
        out_weight.reshape(4, 2, 64, 2048),
        master_gate.reshape(shape5), master_up.reshape(shape5), master_down.reshape(shape5),
    )
    return out.astype(BF).reshape(4, 16, 2048)


def solution(mesh):
    return jax.shard_map(
        per_device,
        mesh=mesh,
        in_specs=(
            P(None, ("fsdp", "expert"), None),
            P(("fsdp", "expert"), None, None),
            P(("fsdp", "expert"), None, None),
            P(("fsdp", "expert")),
            P(None, ("fsdp", "expert"), None),
            P(None, ("fsdp", "expert"), None),
            P(None, ("fsdp", "expert"), None),
            P("fsdp", None),
            P(),
            P(),
            P(None, ("fsdp", "expert"), None),
            P("fsdp", "expert", None),
            P("fsdp", "expert", None),
            P("fsdp", "expert", None),
        ),
        out_specs=P(None, ("fsdp", "expert"), None),
        check_vma=False,
    )
```

```python
import functools
import math

import jax
import jax.numpy as jnp
from jax import lax
from jax.experimental import pallas as pl
from jax.experimental.pallas import tpu as pltpu
from jax.sharding import PartitionSpec as P

MESH = pl.DeviceIdType.MESH
BF = jnp.bfloat16
F32 = jnp.float32
NT = (((1,), (1,)), ((), ()))
TN = (((0,), (0,)), ((), ()))
DEPTH = 8
UNROLL = 4
G_AT, U_AT = 5, 5


def dot(a, b):
    return jnp.dot(a, b, preferred_element_type=F32)


def dot_nt(a, b):
    return lax.dot_general(a, b, NT, preferred_element_type=F32)


def dot_tn(a, b):
    return lax.dot_general(a, b, TN, preferred_element_type=F32)


def kernel(
    x_ref, q_ref, nk_ref, nv_ref, gain_ref, ids_ref, len_ref,
    ck_hbm, cv_hbm, router_hbm, wo_ref, mg_ref, mu_ref, md_ref,
    out_ref,
    ck_ref, cv_ref, router_ref, stage, ws, mid_a, mid_b, wgu, wd, wout, ag_a, ag_b, ssend, srecv,
    o_s, nk_s, nv_s, att, attr, resid, pg, rs1, rs2,
    st_sem, in_sem, w1_s, w1_r, d1_s, d1_r, w2_s, w2_r, d2_s, d2_r, own_sem, o_snd, o_rcv, f_snd, f_rcv, one_sem,
    ag_s, ag_r, z_s, z_r, t_s, t_r, r1_s, r1_r, r2_s, r2_r,
):
    z = lax.axis_index("fsdp")
    e = lax.axis_index("expert")
    x = e // 8
    y = (e // 2) % 4
    c = e % 2
    me = z * 2 + c

    def dev(dx=0, dy=0, dc=0, dz=0):
        return (
            (z + dz) % 4,
            ((x + dx) % 4) * 8 + ((y + dy) % 4) * 2 + (c + dc) % 2,
        )

    def remote(src, dst, snd, rcv, target):
        return pltpu.make_async_remote_copy(
            src_ref=src, dst_ref=dst, send_sem=snd, recv_sem=rcv,
            device_id=target, device_id_type=MESH,
        )

    masters = (mg_ref, mu_ref, md_ref)

    def load(t, j, slot):
        return pltpu.make_async_copy(masters[t].at[j // 4, j % 4], stage.at[slot], st_sem.at[slot])

    for j in range(DEPTH):
        load(0, j, j).start()
    own_out = pltpu.make_async_copy(wo_ref, wout.at[pl.ds(0, 4)], own_sem)
    own_out.start()
    local_ins = [
        pltpu.make_async_copy(src, dst, in_sem.at[i])
        for i, (src, dst) in enumerate(
            ((ck_hbm, ck_ref), (cv_hbm, cv_ref), (router_hbm, router_ref))
        )
    ]
    for cp in local_ins:
        cp.start()

    partners = [(d, 0, k, 0) for d in (1, 2, 3) for k in (0, 1)]
    partners += [(0, d, k, 0) for d in (1, 2, 3) for k in (0, 1)]
    partners += [(0, 0, k, d) for d in (1, 2, 3) for k in (0, 1)]
    partners += [(0, 0, 1, 0)]
    barrier = pltpu.get_barrier_semaphore()
    for p in partners:
        pl.semaphore_signal(barrier, inc=1, device_id=dev(*p), device_id_type=MESH)
    pl.semaphore_wait(barrier, len(partners))

    drains = []

    def cast(t):
        def one(j):
            slot = j % DEPTH
            load(t, j, slot).wait()
            ws[t, j // 4, j % 4] = stage[slot].astype(BF)
            return slot

        def step_a(j, carry):
            load(t, j + DEPTH, one(j)).start()
            return carry

        def step_b(j, carry):
            slot = one(j)
            if t < 2:
                load(t + 1, j + DEPTH - 16, slot).start()
            return carry

        lax.fori_loop(0, 16 - DEPTH, step_a, 0)
        lax.fori_loop(16 - DEPTH, 16, step_b, 0)

    def leg_one(t, k=None):
        group = []
        snd, rcv = (w1_s.at[t], w1_r.at[t]) if k is None else (d1_s.at[k], d1_r.at[k])
        rows = pl.ds(0, 64) if k is None else pl.ds(k * 16, 16)
        for d in (2, 1, 3, 0):
            for dc in (0, 1):
                i = d * 2 + dc
                xd, yd, cd = (x + d) % 4, (y + d) % 4, (c + dc) % 2
                src_a = ws.at[t, xd, :, cd, rows, pl.ds(0, 384)]
                src_b = ws.at[t, :, yd, cd, rows, pl.ds(384, 384)]
                dst_a, dst_b = mid_a.at[t, x, c, :, rows], mid_b.at[t, y, c, :, rows]
                if i == 0:
                    cp_a = pltpu.make_async_copy(src_a, dst_a, rcv.at[0, i])
                    cp_b = pltpu.make_async_copy(src_b, dst_b, rcv.at[1, i])
                else:
                    cp_a = remote(
                        src_a, dst_a, snd.at[0, i], rcv.at[0, i], dev(dx=d, dc=dc)
                    )
                    cp_b = remote(
                        src_b, dst_b, snd.at[1, i], rcv.at[1, i], dev(dy=d, dc=dc)
                    )
                    drains.extend([cp_a, cp_b])
                cp_a.start()
                cp_b.start()
                group += [(i, cp_a), (i, cp_b)]
        return group

    def wait_group(group):
        for i, cp in group:
            if i == 0:
                cp.wait()
            else:
                cp.wait_recv()

    def second(t, k):
        group = []
        for d in (2, 1, 3, 0):
            xd, yd = (x + d) % 4, (y + d) % 4
            if k is None:
                src_a, src_b = mid_a.at[t, :, :, yd], mid_b.at[t, :, :, xd]
                dst_a = wgu.at[t, :, y, :, :, pl.ds(0, 384)]
                dst_b = wgu.at[t, x, :, :, :, pl.ds(384, 384)]
                snd, rcv = w2_s.at[t], w2_r.at[t]
            else:
                src_a = mid_a.at[t, :, :, yd, pl.ds(16 * k, 16)]
                src_b = mid_b.at[t, :, :, xd, pl.ds(16 * k, 16)]
                dst_a = wd.at[k, :, y, :, :, pl.ds(0, 384)]
                dst_b = wd.at[k, x, :, :, :, pl.ds(384, 384)]
                snd, rcv = d2_s.at[k], d2_r.at[k]
            if d == 0:
                cp_a = pltpu.make_async_copy(src_a, dst_a, rcv.at[0, 0])
                cp_b = pltpu.make_async_copy(src_b, dst_b, rcv.at[1, 0])
            else:
                cp_a = remote(src_a, dst_a, snd.at[0, d], rcv.at[0, d], dev(dy=d))
                cp_b = remote(src_b, dst_b, snd.at[1, d], rcv.at[1, d], dev(dx=d))
                drains.extend([cp_a, cp_b])
            cp_a.start()
            cp_b.start()
            group += [(d, cp_a), (d, cp_b)]
        return group

    cast(0)
    first = [leg_one(0)]
    cast(1)
    first.append(leg_one(1))
    for cp in local_ins:
        cp.wait()

    inv = 1.0 / math.sqrt(128.0)
    neg = -jnp.inf
    lane = lax.broadcasted_iota(jnp.int32, (32, 136), 1)
    fresh_ok = (lane >= 128) & (
        lane - 128 <= (lax.broadcasted_iota(jnp.int32, (32, 136), 0) >> 3)
    )
    for g in range(2):
        for h in range(8):
            for t in range(4):
                head = g * 8 + h
                o_s[:, g, t * 8 + h, :] = q_ref[t, :, head * 128:(head + 1) * 128].astype(F32)
    for s in range(8):
        if s < 4:
            nk_s[:, s, :] = nk_ref[s].astype(F32)
            nv_s[:, s, :] = nv_ref[s].astype(F32)
        else:
            nk_s[:, s, :] = jnp.zeros((16, 256), F32)
            nv_s[:, s, :] = jnp.zeros((16, 256), F32)
    def attend(r, carry):
        ok = fresh_ok | (lane < len_ref[r])
        for g in range(2):
            cols = slice(g * 128, (g + 1) * 128)
            qq = o_s[r, g].astype(BF)
            keys = jnp.concatenate([ck_ref[r, :, cols], nk_s[r, :, cols].astype(BF)], axis=0)
            values = jnp.concatenate([cv_ref[r, :, cols], nv_s[r, :, cols].astype(BF)], axis=0)
            s = jnp.where(ok, dot_nt(qq, keys) * inv, neg)
            es = jnp.exp(s - jnp.max(s, axis=-1, keepdims=True))
            ps = (es / jnp.sum(es, axis=-1, keepdims=True)).astype(BF)
            o_s[r, g] = dot(ps, values)
        return carry

    def attend_some(i, carry):
        for j in range(UNROLL):
            attend(i * UNROLL + j, 0)
        return carry

    lax.fori_loop(0, 16 // UNROLL, attend_some, 0)
    for g in range(2):
        for h in range(8):
            for t in range(4):
                head = g * 8 + h
                att[t * 16:(t + 1) * 16, head * 128:(head + 1) * 128] = o_s[
                    :, g, t * 8 + h, :
                ].astype(BF)

    toward = []
    for dz in (1, 3, 2):
        to = (z + dz) % 4
        cols = pl.ds(pl.multiple_of(to * 512, 512), 512)
        cp = remote(att.at[:, cols], attr.at[z], o_snd.at[dz - 1], o_rcv.at[dz - 1], dev(dz=dz))
        cp.start()
        toward.append(cp)
    mine = pltpu.make_async_copy(
        att.at[:, pl.ds(pl.multiple_of(z * 512, 512), 512)], attr.at[z], one_sem
    )
    mine.start()
    mine.wait()
    own_out.wait()
    for cp in toward:
        cp.wait()

    def project(n, carry):
        cols = pl.ds(pl.multiple_of(n * 512, 512), 512)
        got = dot(attr[...].reshape(256, 512), wout[0:4, :, :, cols].reshape(512, 512))
        ssend[0:4, 0, :, cols] = got.astype(BF).reshape(4, 64, 512)
        return carry

    lax.fori_loop(0, 4, project, 0)
    partial = []
    for t in range(4):
        rows = pl.ds(t * 16, 16)
        group = []
        for dz in (1, 3, 2):
            cp = remote(
                ssend.at[(z + dz) % 4, 0, rows], rs2.at[dz - 1, rows],
                f_snd.at[t, dz - 1], f_rcv.at[t, dz - 1], dev(dz=dz),
            )
            cp.start()
            group.append(cp)
        partial.append(group)

    def project_own(n, carry):
        cols = pl.ds(pl.multiple_of(n * 512, 512), 512)
        got = dot(attr[z], wout[0:4, :, :, cols].reshape(512, 512))
        resid[:, cols] = x_ref[:, cols].astype(F32) + got
        return carry

    lax.fori_loop(0, 4, project_own, 0)
    cast(2)

    expert_i = lax.broadcasted_iota(jnp.int32, (128, 16), 0)
    row_i = lax.broadcasted_iota(jnp.int32, (16, 16), 0)
    col_i = lax.broadcasted_iota(jnp.int32, (16, 16), 1)
    eye = (row_i == col_i).astype(F32).astype(BF)
    before = (col_i < row_i).astype(F32).astype(BF)
    gain = gain_ref[...].astype(F32).reshape(1, 2048)
    ag1 = []

    def gather_one(t):
        for cp in partial[t]:
            cp.wait()
        span = slice(t * 16, t * 16 + 16)
        res = resid[span, :]
        for d in range(3):
            res = res + rs2[d, span, :].astype(F32)
        resid[span, :] = res
        mean_square = jnp.mean(res * res, axis=-1, keepdims=True)
        normed = (res * lax.rsqrt(mean_square + 1e-06) * gain).astype(BF)
        ag_a[y, x, span, 0:1024] = normed[:, 0:1024]
        ag_b[x, y, span, :] = normed[:, 1024:2048]
        logits = dot(normed, router_ref[...])
        named = jnp.zeros((128, 16), F32)
        for k in range(8):
            named = named + (ids_ref[t, k:k + 1, :] == expert_i).astype(F32)
        member = dot_nt(eye, named.astype(BF))
        rank = dot(before, member.astype(BF))
        chosen = jnp.where(member > 0.5, logits, neg)
        chosen_exp = jnp.exp(chosen - jnp.max(chosen, axis=-1, keepdims=True))
        gates = chosen_exp / jnp.sum(chosen_exp, axis=-1, keepdims=True)
        ag_a[y, x, span, 1024:1152] = jnp.where(rank < 0.5, gates, -gates).astype(BF)
        rows = pl.ds(t * 16, 16)
        group = []
        for d in (2, 1, 3):
            part_a, part_b = ag_a.at[y, x, rows], ag_b.at[x, y, rows]
            cp_a = remote(part_a, part_a, ag_s.at[t, 0, d], ag_r.at[t, 0, d], dev(dx=d))
            cp_b = remote(part_b, part_b, ag_s.at[t, 1, d], ag_r.at[t, 1, d], dev(dy=d))
            cp_a.start()
            cp_b.start()
            group += [cp_a, cp_b]
        ag1.append(group)
    ag2, ag3 = [], []

    def gather_two(t):
        rows = pl.ds(t * 16, 16)
        for cp in ag1[t]:
            cp.wait()
        group = []
        for d in (1, 3):
            part_a, part_b = ag_a.at[y, :, rows], ag_b.at[x, :, rows]
            cp_a = remote(part_a, part_a, ag_s.at[t, 2, d], ag_r.at[t, 2, d], dev(dy=d))
            cp_b = remote(part_b, part_b, ag_s.at[t, 3, d], ag_r.at[t, 3, d], dev(dx=d))
            cp_a.start()
            cp_b.start()
            group += [cp_a, cp_b]
        ag2.append(group)

    def gather_three(t):
        rows = pl.ds(t * 16, 16)
        for cp in ag2[t]:
            cp.wait()
        group = []
        for i, d in ((0, 1), (2, 3)):
            half = pl.ds(i, 2)
            part_a = ag_a.at[(y + 4 - d) % 4, half, rows]
            part_b = ag_b.at[(x + 4 - d) % 4, half, rows]
            cp_a = remote(part_a, part_a, ag_s.at[t, 2, i], ag_r.at[t, 2, i], dev(dy=d))
            cp_b = remote(part_b, part_b, ag_s.at[t, 3, i], ag_r.at[t, 3, i], dev(dx=d))
            cp_a.start()
            cp_b.start()
            group += [cp_a, cp_b]
        ag3.append(group)

    e_row = lax.broadcasted_iota(jnp.int32, (8, 128), 0)
    e_lane = lax.broadcasted_iota(jnp.int32, (8, 128), 1)
    pick = (e_lane == (e_row >> 1) * 32 + (e_row & 1) + x * 8 + y * 2).astype(F32).astype(BF)
    slot_i = lax.broadcasted_iota(jnp.int32, (8, 32, 256), 1)
    row_of = lax.broadcasted_iota(jnp.int32, (8, 32, 256), 2)
    same = (row_of >> 4) == (slot_i >> 1)
    sign = jnp.where((slot_i & 1) == 0, 1.0, -1.0).astype(F32)

    def select(t):
        rows = slice(t * 16, t * 16 + 16)
        dst = slice((t % 2) * 32, (t % 2) * 32 + 32)
        aux = ag_a[:, :, rows, 1024:1152].reshape(256, 128)
        code = dot_nt(pick, aux)
        signed = jnp.where(same, code[:, None, :] * sign, 0.0)
        weight = jnp.maximum(signed, 0.0).reshape(256, 256)
        pg[t] = weight.astype(BF)
        place = (weight > 0.0).astype(F32).astype(BF)
        for n in range(2):
            cols = slice(n * 512, (n + 1) * 512)
            got = dot(place, ag_a[:, :, rows, cols].reshape(256, 512))
            ssend[:, t // 2, dst, cols] = got.astype(BF).reshape(8, 32, 512)
        for n in range(2):
            cols = slice(n * 512, (n + 1) * 512)
            part = jnp.concatenate(
                [ag_b[:, k, rows, cols].reshape(64, 512) for k in range(4)], axis=0
            )
            got = dot(place, part)
            ssend[:, t // 2, dst, n * 512 + 1024:n * 512 + 1536] = got.astype(BF).reshape(8, 32, 512)

    column_devs = [(dz, dc) for dz in (2, 1, 3, 0) for dc in (0, 1)]
    def send_slots(t):
        group = []
        for dz, dc in column_devs:
            i = dz * 2 + dc
            to = ((z + dz) % 4) * 2 + (c + dc) % 2
            rows = pl.ds((t % 2) * 32, 32)
            src, dst = ssend.at[to, t // 2, rows], srecv.at[me, t // 2, rows]
            if i == 0:
                cp = pltpu.make_async_copy(src, dst, z_r.at[t, i])
            else:
                cp = remote(src, dst, z_s.at[t, i], z_r.at[t, i], dev(dz=dz, dc=dc))
            cp.start()
            group.append(cp)
        return group

    dispatch = []
    for step in range(7):
        if step < 4:
            gather_one(step)
        if 1 <= step < 5:
            gather_two(step - 1)
        if 2 <= step < 6:
            gather_three(step - 2)
        if step == G_AT:
            wait_group(first[0])
            g2 = second(0, None)
        if step >= 3:
            t = step - 3
            for cp in ag3[t]:
                cp.wait()
            if step == U_AT:
                wait_group(first[1])
                u2 = second(1, None)
            select(t)
            dispatch.append(send_slots(t))

    d1 = [leg_one(2, 0)]
    wait_group(g2)
    d1.append(leg_one(2, 1))
    wait_group(d1[0])
    d2 = [second(2, 0)]
    wait_group(u2)
    d1.append(leg_one(2, 2))

    for t in range(4):
        for cp in dispatch[t]:
            cp.wait()

    def hide_loop(t, carry):
        half = pl.ds(pl.multiple_of((t % 2) * 32, 32), 32)
        rows = srecv[:, t // 2, half, :].reshape(256, 2048)
        gate = dot(rows, wgu[0].reshape(2048, 768))
        up = dot(rows, wgu[1].reshape(2048, 768))
        ag_b[t, :, :, 0:768] = (jax.nn.silu(gate) * up).astype(BF).reshape(4, 64, 768)
        return carry

    lax.fori_loop(0, 2, hide_loop, 0)
    wait_group(d1[1])
    d2.append(second(2, 1))
    d1.append(leg_one(2, 3))
    lax.fori_loop(2, 4, hide_loop, 0)

    pieces = ((0, 0, 4), (1, 0, 4), (2, 0, 4), (3, 0, 2), (3, 2, 2))

    def down(p):
        k, t0, nt = pieces[p]
        cols = slice(k * 512, (k + 1) * 512)
        if t0 == 0:
            wait_group(d2[k])

        def tile(t, carry):
            half = pl.ds(pl.multiple_of((t % 2) * 32, 32), 32)
            hidden = ag_b[t, :, :, 0:768].reshape(256, 768)
            got = dot_nt(hidden, wd[k].reshape(512, 768))
            srecv[:, t // 2, half, cols] = got.astype(BF).reshape(8, 32, 512)
            return carry

        lax.fori_loop(t0, t0 + nt, tile, 0)
        part = pl.ds(t0 // 2, nt // 2)
        group = []
        for dz, dc in column_devs:
            i = dz * 2 + dc
            to = ((z + dz) % 4) * 2 + (c + dc) % 2
            dst = wout.at[me, part, :, pl.ds(k * 512, 512)]
            if i == 0:
                cp = pltpu.make_async_copy(
                    srecv.at[me, part, :, pl.ds(k * 512, 512)], dst, t_r.at[p, i]
                )
            else:
                cp = remote(
                    srecv.at[to, part, :, pl.ds(k * 512, 512)], dst, t_s.at[p, i], t_r.at[p, i],
                    dev(dz=dz, dc=dc),
                )
                drains.append(cp)
            cp.start()
            group.append((i, cp))
        return group

    def combine(p, group):
        k, t0, nt = pieces[p]
        some = pl.ds(t0 * 16, nt * 16)
        wait_group(group)

        def tile(t, carry):
            rows = pl.ds(pl.multiple_of(t * 16, 16), 16)
            src = pl.ds(pl.multiple_of((t % 2) * 32, 32), 32)
            got = wout[0:8, t // 2, src, k * 512:(k + 1) * 512].reshape(256, 512)
            part = dot_tn(pg[t], got).astype(BF)
            wout[8:16, :, rows, k * 512:k * 512 + 256] = part[:, 0:256].reshape(8, 2, 16, 256)
            for yy in range(4):
                for xx in range(4):
                    b = (yy * 4 + xx) * 16
                    wout[8 + xx * 2 + yy // 2, yy % 2, rows, k * 512 + 256:(k + 1) * 512] = part[
                        b:b + 16, 256:512
                    ]
            return carry

        lax.fori_loop(t0, t0 + nt, tile, 0)
        sums = []
        for d in (2, 1, 3):
            xd, yd = (x + d) % 4, (y + d) % 4
            cp_a = remote(
                wout.at[pl.ds(8 + yd * 2, 2), :, some, pl.ds(k * 512, 256)],
                rs1.at[k, 0, d - 1, :, :, some],
                r1_s.at[p, 0, d - 1], r1_r.at[p, 0, d - 1], dev(dy=d),
            )
            cp_b = remote(
                wout.at[pl.ds(8 + xd * 2, 2), :, some, pl.ds(k * 512 + 256, 256)],
                rs1.at[k, 1, d - 1, :, :, some],
                r1_s.at[p, 1, d - 1], r1_r.at[p, 1, d - 1], dev(dx=d),
            )
            cp_a.start()
            cp_b.start()
            sums += [cp_a, cp_b]
        drains.extend(sums)
        return sums

    def halfway(p, sums):
        k, t0, nt = pieces[p]
        n = nt * 16
        span, some = slice(t0 * 16, t0 * 16 + n), pl.ds(t0 * 16, n)
        for cp in sums:
            cp.wait_recv()
        for route in range(2):
            mine = (y, x)[route]
            lanes = slice(k * 512 + route * 256, k * 512 + route * 256 + 256)
            total = wout[pl.ds(8 + mine * 2, 2), :, span, lanes].reshape(4 * n, 256).astype(F32)
            for d in range(3):
                total = total + rs1[k, route, d, :, :, span, :].reshape(4 * n, 256).astype(F32)
            ag_a[k, :, span, route * 256:(route + 1) * 256] = total.astype(BF).reshape(4, n, 256)
        group = []
        for d in (2, 1, 3):
            xd, yd = (x + d) % 4, (y + d) % 4
            cp_a = remote(
                ag_a.at[k, xd, some, pl.ds(0, 256)],
                rs2.at[d - 1, some, pl.ds(k * 512, 256)],
                r2_s.at[p, 0, d - 1], r2_r.at[p, 0, d - 1], dev(dx=d),
            )
            cp_b = remote(
                ag_a.at[k, yd, some, pl.ds(256, 256)],
                rs2.at[d - 1, some, pl.ds(k * 512 + 256, 256)],
                r2_s.at[p, 1, d - 1], r2_r.at[p, 1, d - 1], dev(dy=d),
            )
            cp_a.start()
            cp_b.start()
            group += [cp_a, cp_b]
        drains.extend(group)
        return group

    def close(p, group):
        k, t0, nt = pieces[p]
        n = nt * 16
        span = slice(t0 * 16, t0 * 16 + n)
        for cp in group:
            cp.wait_recv()
        for route in range(2):
            mine = (x, y)[route]
            total = ag_a[k, mine, span, route * 256:(route + 1) * 256].astype(F32)
            cols = slice(k * 512 + route * 256, k * 512 + (route + 1) * 256)
            for d in range(3):
                total = total + rs2[d, span, cols].astype(F32)
            for i in range(2):
                o_s[k * 4 + route * 2 + i, t0 // 2:(t0 + nt) // 2] = total[
                    :, i * 128:(i + 1) * 128
                ].reshape(nt // 2, 32, 128)

    backs, sums, ends = {}, {}, {}
    for k in range(8):
        if k == 4:
            early = drains[:]
            drains.clear()
        if k < 5:
            backs[k] = down(k)
        if k < 2:
            wait_group(d1[k + 2])
            d2.append(second(2, k + 2))
        if k == 4:
            for cp in early:
                cp.wait_send()
        if 0 <= k - 1 < 5:
            sums[k - 1] = combine(k - 1, backs[k - 1])
        if 0 <= k - 2 < 5:
            ends[k - 2] = halfway(k - 2, sums[k - 2])
        if 0 <= k - 3 < 5:
            close(k - 3, ends[k - 3])

    p_i = lax.broadcasted_iota(jnp.int32, (512, 512), 0)
    o_i = lax.broadcasted_iota(jnp.int32, (512, 512), 1)
    perm = (o_i == ((p_i >> 4) & 7) * 64 + (p_i >> 7) * 16 + (p_i & 15)).astype(F32).astype(BF)
    for g in range(4):
        v = jnp.concatenate(
            [o_s[k * 4 + g].reshape(64, 128) for k in range(4)], axis=1
        )
        hi = v.astype(BF)
        lo = (v - hi.astype(F32)).astype(BF)
        out_ref[:, g * 512:(g + 1) * 512] = (
            resid[:, g * 512:(g + 1) * 512] + dot(hi, perm) + dot(lo, perm)
        ).astype(BF)
    for cp in drains:
        cp.wait_send()


def per_device(
    inputs, cache_keys, cache_values, lengths, new_keys, new_values, queries, out_weight,
    norm_gain, router, experts, master_gate, master_up, master_down,
):
    vm = pl.BlockSpec(memory_space=pltpu.VMEM)
    anyspace = pl.BlockSpec(memory_space=pl.ANY)
    dma = pltpu.SemaphoreType.DMA
    shape5 = (4, 4, 2, 64, 768)
    out = pl.pallas_call(
        kernel,
        out_shape=jax.ShapeDtypeStruct((64, 2048), BF),
        in_specs=[vm] * 6 + [pl.BlockSpec(memory_space=pltpu.SMEM)] + [anyspace] * 7,
        out_specs=vm,
        scratch_shapes=[
            pltpu.VMEM((16, 128, 256), BF),
            pltpu.VMEM((16, 128, 256), BF),
            pltpu.VMEM((2048, 128), BF),
            pltpu.VMEM((DEPTH, 2, 64, 768), F32),
            pltpu.VMEM((3, 4, 4, 2, 64, 768), BF),
            pltpu.VMEM((3, 4, 2, 4, 64, 384), BF),
            pltpu.VMEM((3, 4, 2, 4, 64, 384), BF),
            pltpu.VMEM((2, 4, 4, 2, 64, 768), BF),
            pltpu.VMEM((4, 4, 4, 2, 16, 768), BF),
            pltpu.VMEM((16, 2, 64, 2048), BF),
            pltpu.VMEM((4, 4, 64, 1152), BF),
            pltpu.VMEM((4, 4, 64, 1024), BF),
            pltpu.VMEM((8, 2, 64, 2048), BF),
            pltpu.VMEM((8, 2, 64, 2048), BF),
            pltpu.VMEM((16, 2, 32, 128), F32),
            pltpu.VMEM((16, 8, 256), F32),
            pltpu.VMEM((16, 8, 256), F32),
            pltpu.VMEM((64, 2048), BF),
            pltpu.VMEM((4, 64, 512), BF),
            pltpu.VMEM((64, 2048), F32),
            pltpu.VMEM((4, 256, 256), BF),
            pltpu.VMEM((4, 2, 3, 2, 2, 64, 256), BF),
            pltpu.VMEM((3, 64, 2048), BF),
            dma((DEPTH,)),
            dma((3,)), dma((2, 2, 8)), dma((2, 2, 8)), dma((4, 2, 8)), dma((4, 2, 8)),
            dma((2, 2, 4)), dma((2, 2, 4)),
            dma((4, 2, 4)), dma((4, 2, 4)),
            dma, dma((3,)), dma((3,)), dma((4, 3)), dma((4, 3)), dma,
            dma((4, 4, 4)), dma((4, 4, 4)),
            dma((4, 8)), dma((4, 8)),
            dma((5, 8)), dma((5, 8)),
            dma((5, 2, 3)), dma((5, 2, 3)),
            dma((5, 2, 3)), dma((5, 2, 3)),
        ],
        compiler_params=pltpu.CompilerParams(
            collective_id=0, has_side_effects=True, vmem_limit_bytes=66_900_000
        ),
        name="moe_decode",
    )(
        inputs.reshape(64, 2048), queries, new_keys, new_values,
        norm_gain, experts.transpose(0, 2, 1), lengths, cache_keys, cache_values, router,
        out_weight.reshape(4, 2, 64, 2048),
        master_gate.reshape(shape5), master_up.reshape(shape5), master_down.reshape(shape5),
    )
    return out.reshape(4, 16, 2048)


def solution(mesh):
    return jax.shard_map(
        per_device,
        mesh=mesh,
        in_specs=(
            P(None, ("fsdp", "expert"), None),
            P(("fsdp", "expert"), None, None),
            P(("fsdp", "expert"), None, None),
            P(("fsdp", "expert")),
            P(None, ("fsdp", "expert"), None),
            P(None, ("fsdp", "expert"), None),
            P(None, ("fsdp", "expert"), None),
            P("fsdp", None),
            P(),
            P(),
            P(None, ("fsdp", "expert"), None),
            P("fsdp", "expert", None),
            P("fsdp", "expert", None),
            P("fsdp", "expert", None),
        ),
        out_specs=P(None, ("fsdp", "expert"), None),
        check_vma=False,
    )
```

```python
import functools
import math

import jax
import jax.numpy as jnp
from jax import lax
from jax.experimental import pallas as pl
from jax.experimental.pallas import tpu as pltpu
from jax.sharding import PartitionSpec as P

MESH = pl.DeviceIdType.MESH
BF = jnp.bfloat16
F32 = jnp.float32
NT = (((1,), (1,)), ((), ()))
TN = (((0,), (0,)), ((), ()))
DEPTH = 8
UNROLL = 4
G_AT, U_AT = 5, 5


def dot(a, b):
    return jnp.dot(a, b, preferred_element_type=F32)


def dot_nt(a, b):
    return lax.dot_general(a, b, NT, preferred_element_type=F32)


def dot_tn(a, b):
    return lax.dot_general(a, b, TN, preferred_element_type=F32)


def kernel(
    x_ref, q_ref, nk_ref, nv_ref, gain_ref, ids_ref, len_ref,
    ck_hbm, cv_hbm, router_hbm, wo_ref, mg_ref, mu_ref, md_ref,
    out_ref,
    ck_ref, cv_ref, router_ref, stage, ws, mid_a, mid_b, wgu, wd, wout, ag_a, ag_b, ssend, srecv,
    o_s, nk_s, nv_s, att, attr, resid, pg, rs1, rs2,
    st_sem, in_sem, w1_s, w1_r, d1_s, d1_r, w2_s, w2_r, d2_s, d2_r, own_sem, o_snd, o_rcv, f_snd, f_rcv, one_sem,
    ag_s, ag_r, z_s, z_r, t_s, t_r, r1_s, r1_r, r2_s, r2_r,
):
    z = lax.axis_index("fsdp")
    e = lax.axis_index("expert")
    x = e // 8
    y = (e // 2) % 4
    c = e % 2
    me = z * 2 + c

    def dev(dx=0, dy=0, dc=0, dz=0):
        return (
            (z + dz) % 4,
            ((x + dx) % 4) * 8 + ((y + dy) % 4) * 2 + (c + dc) % 2,
        )

    def remote(src, dst, snd, rcv, target):
        return pltpu.make_async_remote_copy(
            src_ref=src, dst_ref=dst, send_sem=snd, recv_sem=rcv,
            device_id=target, device_id_type=MESH,
        )

    masters = (mg_ref, mu_ref, md_ref)

    def load(t, j, slot):
        return pltpu.make_async_copy(masters[t].at[j // 4, j % 4], stage.at[slot], st_sem.at[slot])

    for j in range(DEPTH):
        load(0, j, j).start()
    own_out = pltpu.make_async_copy(wo_ref, wout.at[pl.ds(0, 4)], own_sem)
    own_out.start()
    local_ins = [
        pltpu.make_async_copy(src, dst, in_sem.at[i])
        for i, (src, dst) in enumerate(
            ((ck_hbm, ck_ref), (cv_hbm, cv_ref), (router_hbm, router_ref))
        )
    ]
    for cp in local_ins:
        cp.start()

    partners = [(d, 0, k, 0) for d in (1, 2, 3) for k in (0, 1)]
    partners += [(0, d, k, 0) for d in (1, 2, 3) for k in (0, 1)]
    partners += [(0, 0, k, d) for d in (1, 2, 3) for k in (0, 1)]
    partners += [(0, 0, 1, 0)]
    barrier = pltpu.get_barrier_semaphore()
    for p in partners:
        pl.semaphore_signal(barrier, inc=1, device_id=dev(*p), device_id_type=MESH)
    pl.semaphore_wait(barrier, len(partners))

    drains = []

    def cast(t):
        def one(j):
            slot = j % DEPTH
            load(t, j, slot).wait()
            ws[t, j // 4, j % 4] = stage[slot].astype(BF)
            return slot

        def step_a(j, carry):
            load(t, j + DEPTH, one(j)).start()
            return carry

        def step_b(j, carry):
            slot = one(j)
            if t < 2:
                load(t + 1, j + DEPTH - 16, slot).start()
            return carry

        lax.fori_loop(0, 16 - DEPTH, step_a, 0)
        lax.fori_loop(16 - DEPTH, 16, step_b, 0)

    def leg_one(t, k=None):
        group = []
        snd, rcv = (w1_s.at[t], w1_r.at[t]) if k is None else (d1_s.at[k], d1_r.at[k])
        rows = pl.ds(0, 64) if k is None else pl.ds(k * 16, 16)
        for d in (2, 1, 3, 0):
            for dc in (0, 1):
                i = d * 2 + dc
                xd, yd, cd = (x + d) % 4, (y + d) % 4, (c + dc) % 2
                src_a = ws.at[t, xd, :, cd, rows, pl.ds(0, 384)]
                src_b = ws.at[t, :, yd, cd, rows, pl.ds(384, 384)]
                dst_a, dst_b = mid_a.at[t, x, c, :, rows], mid_b.at[t, y, c, :, rows]
                if i == 0:
                    cp_a = pltpu.make_async_copy(src_a, dst_a, rcv.at[0, i])
                    cp_b = pltpu.make_async_copy(src_b, dst_b, rcv.at[1, i])
                else:
                    cp_a = remote(
                        src_a, dst_a, snd.at[0, i], rcv.at[0, i], dev(dx=d, dc=dc)
                    )
                    cp_b = remote(
                        src_b, dst_b, snd.at[1, i], rcv.at[1, i], dev(dy=d, dc=dc)
                    )
                    drains.extend([cp_a, cp_b])
                cp_a.start()
                cp_b.start()
                group += [(i, cp_a), (i, cp_b)]
        return group

    def wait_group(group):
        for i, cp in group:
            if i == 0:
                cp.wait()
            else:
                cp.wait_recv()

    def second(t, k):
        group = []
        for d in (2, 1, 3, 0):
            xd, yd = (x + d) % 4, (y + d) % 4
            if k is None:
                src_a, src_b = mid_a.at[t, :, :, yd], mid_b.at[t, :, :, xd]
                dst_a = wgu.at[t, :, y, :, :, pl.ds(0, 384)]
                dst_b = wgu.at[t, x, :, :, :, pl.ds(384, 384)]
                snd, rcv = w2_s.at[t], w2_r.at[t]
            else:
                src_a = mid_a.at[t, :, :, yd, pl.ds(16 * k, 16)]
                src_b = mid_b.at[t, :, :, xd, pl.ds(16 * k, 16)]
                dst_a = wd.at[k, :, y, :, :, pl.ds(0, 384)]
                dst_b = wd.at[k, x, :, :, :, pl.ds(384, 384)]
                snd, rcv = d2_s.at[k], d2_r.at[k]
            if d == 0:
                cp_a = pltpu.make_async_copy(src_a, dst_a, rcv.at[0, 0])
                cp_b = pltpu.make_async_copy(src_b, dst_b, rcv.at[1, 0])
            else:
                cp_a = remote(src_a, dst_a, snd.at[0, d], rcv.at[0, d], dev(dy=d))
                cp_b = remote(src_b, dst_b, snd.at[1, d], rcv.at[1, d], dev(dx=d))
                drains.extend([cp_a, cp_b])
            cp_a.start()
            cp_b.start()
            group += [(d, cp_a), (d, cp_b)]
        return group

    cast(0)
    first = [leg_one(0)]
    cast(1)
    first.append(leg_one(1))
    for cp in local_ins:
        cp.wait()

    inv = 1.0 / math.sqrt(128.0)
    neg = -jnp.inf
    lane = lax.broadcasted_iota(jnp.int32, (32, 136), 1)
    fresh_ok = (lane >= 128) & (
        lane - 128 <= (lax.broadcasted_iota(jnp.int32, (32, 136), 0) >> 3)
    )
    for g in range(2):
        for h in range(8):
            for t in range(4):
                head = g * 8 + h
                o_s[:, g, t * 8 + h, :] = q_ref[t, :, head * 128:(head + 1) * 128].astype(F32)
    for s in range(8):
        if s < 4:
            nk_s[:, s, :] = nk_ref[s].astype(F32)
            nv_s[:, s, :] = nv_ref[s].astype(F32)
        else:
            nk_s[:, s, :] = jnp.zeros((16, 256), F32)
            nv_s[:, s, :] = jnp.zeros((16, 256), F32)
    def attend(r, carry):
        ok = fresh_ok | (lane < len_ref[r])
        for g in range(2):
            cols = slice(g * 128, (g + 1) * 128)
            qq = o_s[r, g].astype(BF)
            keys = jnp.concatenate([ck_ref[r, :, cols], nk_s[r, :, cols].astype(BF)], axis=0)
            values = jnp.concatenate([cv_ref[r, :, cols], nv_s[r, :, cols].astype(BF)], axis=0)
            s = jnp.where(ok, dot_nt(qq, keys) * inv, neg)
            es = jnp.exp(s - jnp.max(s, axis=-1, keepdims=True))
            ps = (es / jnp.sum(es, axis=-1, keepdims=True)).astype(BF)
            o_s[r, g] = dot(ps, values)
        return carry

    def attend_some(i, carry):
        for j in range(UNROLL):
            attend(i * UNROLL + j, 0)
        return carry

    lax.fori_loop(0, 16 // UNROLL, attend_some, 0)
    for g in range(2):
        for h in range(8):
            for t in range(4):
                head = g * 8 + h
                att[t * 16:(t + 1) * 16, head * 128:(head + 1) * 128] = o_s[
                    :, g, t * 8 + h, :
                ].astype(BF)

    toward = []
    for dz in (2, 1, 3):
        to = (z + dz) % 4
        cols = pl.ds(pl.multiple_of(to * 512, 512), 512)
        cp = remote(att.at[:, cols], attr.at[z], o_snd.at[dz - 1], o_rcv.at[dz - 1], dev(dz=dz))
        cp.start()
        toward.append(cp)
    mine = pltpu.make_async_copy(
        att.at[:, pl.ds(pl.multiple_of(z * 512, 512), 512)], attr.at[z], one_sem
    )
    mine.start()
    mine.wait()
    own_out.wait()
    for cp in toward:
        cp.wait()

    def project(n, carry):
        cols = pl.ds(pl.multiple_of(n * 512, 512), 512)
        got = dot(attr[...].reshape(256, 512), wout[0:4, :, :, cols].reshape(512, 512))
        ssend[0:4, 0, :, cols] = got.astype(BF).reshape(4, 64, 512)
        return carry

    lax.fori_loop(0, 4, project, 0)
    partial = []
    for t in range(4):
        rows = pl.ds(t * 16, 16)
        group = []
        for dz in (2, 1, 3):
            cp = remote(
                ssend.at[(z + dz) % 4, 0, rows], rs2.at[dz - 1, rows],
                f_snd.at[t, dz - 1], f_rcv.at[t, dz - 1], dev(dz=dz),
            )
            cp.start()
            group.append(cp)
        partial.append(group)

    def project_own(n, carry):
        cols = pl.ds(pl.multiple_of(n * 512, 512), 512)
        got = dot(attr[z], wout[0:4, :, :, cols].reshape(512, 512))
        resid[:, cols] = x_ref[:, cols].astype(F32) + got
        return carry

    lax.fori_loop(0, 4, project_own, 0)
    cast(2)

    expert_i = lax.broadcasted_iota(jnp.int32, (128, 16), 0)
    row_i = lax.broadcasted_iota(jnp.int32, (16, 16), 0)
    col_i = lax.broadcasted_iota(jnp.int32, (16, 16), 1)
    eye = (row_i == col_i).astype(F32).astype(BF)
    before = (col_i < row_i).astype(F32).astype(BF)
    gain = gain_ref[...].astype(F32).reshape(1, 2048)
    ag1 = []

    def gather_one(t):
        for cp in partial[t]:
            cp.wait()
        span = slice(t * 16, t * 16 + 16)
        res = resid[span, :]
        for d in range(3):
            res = res + rs2[d, span, :].astype(F32)
        resid[span, :] = res
        mean_square = jnp.mean(res * res, axis=-1, keepdims=True)
        normed = (res * lax.rsqrt(mean_square + 1e-06) * gain).astype(BF)
        ag_a[y, x, span, 0:1024] = normed[:, 0:1024]
        ag_b[x, y, span, :] = normed[:, 1024:2048]
        logits = dot(normed, router_ref[...])
        named = jnp.zeros((128, 16), F32)
        for k in range(8):
            named = named + (ids_ref[t, k:k + 1, :] == expert_i).astype(F32)
        member = dot_nt(eye, named.astype(BF))
        rank = dot(before, member.astype(BF))
        chosen = jnp.where(member > 0.5, logits, neg)
        chosen_exp = jnp.exp(chosen - jnp.max(chosen, axis=-1, keepdims=True))
        gates = chosen_exp / jnp.sum(chosen_exp, axis=-1, keepdims=True)
        ag_a[y, x, span, 1024:1152] = jnp.where(rank < 0.5, gates, -gates).astype(BF)
        rows = pl.ds(t * 16, 16)
        group = []
        for d in (2, 1, 3):
            part_a, part_b = ag_a.at[y, x, rows], ag_b.at[x, y, rows]
            cp_a = remote(part_a, part_a, ag_s.at[t, 0, d], ag_r.at[t, 0, d], dev(dx=d))
            cp_b = remote(part_b, part_b, ag_s.at[t, 1, d], ag_r.at[t, 1, d], dev(dy=d))
            cp_a.start()
            cp_b.start()
            group += [cp_a, cp_b]
        ag1.append(group)
    ag2, ag3 = [], []

    def gather_two(t):
        rows = pl.ds(t * 16, 16)
        for cp in ag1[t]:
            cp.wait()
        group = []
        for d in (1, 3):
            part_a, part_b = ag_a.at[y, :, rows], ag_b.at[x, :, rows]
            cp_a = remote(part_a, part_a, ag_s.at[t, 2, d], ag_r.at[t, 2, d], dev(dy=d))
            cp_b = remote(part_b, part_b, ag_s.at[t, 3, d], ag_r.at[t, 3, d], dev(dx=d))
            cp_a.start()
            cp_b.start()
            group += [cp_a, cp_b]
        ag2.append(group)

    def gather_three(t):
        rows = pl.ds(t * 16, 16)
        for cp in ag2[t]:
            cp.wait()
        group = []
        for i, d in ((0, 1), (2, 3)):
            half = pl.ds(i, 2)
            part_a = ag_a.at[(y + 4 - d) % 4, half, rows]
            part_b = ag_b.at[(x + 4 - d) % 4, half, rows]
            cp_a = remote(part_a, part_a, ag_s.at[t, 2, i], ag_r.at[t, 2, i], dev(dy=d))
            cp_b = remote(part_b, part_b, ag_s.at[t, 3, i], ag_r.at[t, 3, i], dev(dx=d))
            cp_a.start()
            cp_b.start()
            group += [cp_a, cp_b]
        ag3.append(group)

    e_row = lax.broadcasted_iota(jnp.int32, (8, 128), 0)
    e_lane = lax.broadcasted_iota(jnp.int32, (8, 128), 1)
    pick = (e_lane == (e_row >> 1) * 32 + (e_row & 1) + x * 8 + y * 2).astype(F32).astype(BF)
    slot_i = lax.broadcasted_iota(jnp.int32, (8, 32, 256), 1)
    row_of = lax.broadcasted_iota(jnp.int32, (8, 32, 256), 2)
    same = (row_of >> 4) == (slot_i >> 1)
    sign = jnp.where((slot_i & 1) == 0, 1.0, -1.0).astype(F32)

    def select(t):
        rows = slice(t * 16, t * 16 + 16)
        dst = slice((t % 2) * 32, (t % 2) * 32 + 32)
        aux = ag_a[:, :, rows, 1024:1152].reshape(256, 128)
        code = dot_nt(pick, aux)
        signed = jnp.where(same, code[:, None, :] * sign, 0.0)
        weight = jnp.maximum(signed, 0.0).reshape(256, 256)
        pg[t] = weight.astype(BF)
        place = (weight > 0.0).astype(F32).astype(BF)
        for n in range(2):
            cols = slice(n * 512, (n + 1) * 512)
            got = dot(place, ag_a[:, :, rows, cols].reshape(256, 512))
            ssend[:, t // 2, dst, cols] = got.astype(BF).reshape(8, 32, 512)
        for n in range(2):
            cols = slice(n * 512, (n + 1) * 512)
            part = jnp.concatenate(
                [ag_b[:, k, rows, cols].reshape(64, 512) for k in range(4)], axis=0
            )
            got = dot(place, part)
            ssend[:, t // 2, dst, n * 512 + 1024:n * 512 + 1536] = got.astype(BF).reshape(8, 32, 512)

    column_devs = [(dz, dc) for dz in (2, 1, 3, 0) for dc in (0, 1)]
    def send_slots(t):
        group = []
        for dz, dc in column_devs:
            i = dz * 2 + dc
            to = ((z + dz) % 4) * 2 + (c + dc) % 2
            rows = pl.ds((t % 2) * 32, 32)
            src, dst = ssend.at[to, t // 2, rows], srecv.at[me, t // 2, rows]
            if i == 0:
                cp = pltpu.make_async_copy(src, dst, z_r.at[t, i])
            else:
                cp = remote(src, dst, z_s.at[t, i], z_r.at[t, i], dev(dz=dz, dc=dc))
            cp.start()
            group.append(cp)
        return group

    dispatch = []
    for step in range(7):
        if step < 4:
            gather_one(step)
        if 1 <= step < 5:
            gather_two(step - 1)
        if 2 <= step < 6:
            gather_three(step - 2)
        if step == G_AT:
            wait_group(first[0])
            g2 = second(0, None)
        if step >= 3:
            t = step - 3
            for cp in ag3[t]:
                cp.wait()
            if step == U_AT:
                wait_group(first[1])
                u2 = second(1, None)
            select(t)
            dispatch.append(send_slots(t))

    d1 = [leg_one(2, 0)]
    wait_group(g2)
    d1.append(leg_one(2, 1))
    wait_group(d1[0])
    d2 = [second(2, 0)]
    wait_group(u2)
    d1.append(leg_one(2, 2))

    for t in range(4):
        for cp in dispatch[t]:
            cp.wait()

    def hide_loop(t, carry):
        half = pl.ds(pl.multiple_of((t % 2) * 32, 32), 32)
        rows = srecv[:, t // 2, half, :].reshape(256, 2048)
        gate = dot(rows, wgu[0].reshape(2048, 768))
        up = dot(rows, wgu[1].reshape(2048, 768))
        ag_b[t, :, :, 0:768] = (jax.nn.silu(gate) * up).astype(BF).reshape(4, 64, 768)
        return carry

    lax.fori_loop(0, 2, hide_loop, 0)
    wait_group(d1[1])
    d2.append(second(2, 1))
    d1.append(leg_one(2, 3))
    lax.fori_loop(2, 4, hide_loop, 0)

    pieces = ((0, 0, 4), (1, 0, 4), (2, 0, 4), (3, 0, 2), (3, 2, 2))

    def down(p):
        k, t0, nt = pieces[p]
        cols = slice(k * 512, (k + 1) * 512)
        if t0 == 0:
            wait_group(d2[k])

        def tile(t, carry):
            half = pl.ds(pl.multiple_of((t % 2) * 32, 32), 32)
            hidden = ag_b[t, :, :, 0:768].reshape(256, 768)
            got = dot_nt(hidden, wd[k].reshape(512, 768))
            srecv[:, t // 2, half, cols] = got.astype(BF).reshape(8, 32, 512)
            return carry

        lax.fori_loop(t0, t0 + nt, tile, 0)
        part = pl.ds(t0 // 2, nt // 2)
        group = []
        for dz, dc in column_devs:
            i = dz * 2 + dc
            to = ((z + dz) % 4) * 2 + (c + dc) % 2
            dst = wout.at[me, part, :, pl.ds(k * 512, 512)]
            if i == 0:
                cp = pltpu.make_async_copy(
                    srecv.at[me, part, :, pl.ds(k * 512, 512)], dst, t_r.at[p, i]
                )
            else:
                cp = remote(
                    srecv.at[to, part, :, pl.ds(k * 512, 512)], dst, t_s.at[p, i], t_r.at[p, i],
                    dev(dz=dz, dc=dc),
                )
                drains.append(cp)
            cp.start()
            group.append((i, cp))
        return group

    def combine(p, group):
        k, t0, nt = pieces[p]
        some = pl.ds(t0 * 16, nt * 16)
        wait_group(group)

        def tile(t, carry):
            rows = pl.ds(pl.multiple_of(t * 16, 16), 16)
            src = pl.ds(pl.multiple_of((t % 2) * 32, 32), 32)
            got = wout[0:8, t // 2, src, k * 512:(k + 1) * 512].reshape(256, 512)
            part = dot_tn(pg[t], got).astype(BF)
            wout[8:16, :, rows, k * 512:k * 512 + 256] = part[:, 0:256].reshape(8, 2, 16, 256)
            for yy in range(4):
                for xx in range(4):
                    b = (yy * 4 + xx) * 16
                    wout[8 + xx * 2 + yy // 2, yy % 2, rows, k * 512 + 256:(k + 1) * 512] = part[
                        b:b + 16, 256:512
                    ]
            return carry

        lax.fori_loop(t0, t0 + nt, tile, 0)
        sums = []
        for d in (2, 1, 3):
            xd, yd = (x + d) % 4, (y + d) % 4
            cp_a = remote(
                wout.at[pl.ds(8 + yd * 2, 2), :, some, pl.ds(k * 512, 256)],
                rs1.at[k, 0, d - 1, :, :, some],
                r1_s.at[p, 0, d - 1], r1_r.at[p, 0, d - 1], dev(dy=d),
            )
            cp_b = remote(
                wout.at[pl.ds(8 + xd * 2, 2), :, some, pl.ds(k * 512 + 256, 256)],
                rs1.at[k, 1, d - 1, :, :, some],
                r1_s.at[p, 1, d - 1], r1_r.at[p, 1, d - 1], dev(dx=d),
            )
            cp_a.start()
            cp_b.start()
            sums += [cp_a, cp_b]
        drains.extend(sums)
        return sums

    def halfway(p, sums):
        k, t0, nt = pieces[p]
        n = nt * 16
        span, some = slice(t0 * 16, t0 * 16 + n), pl.ds(t0 * 16, n)
        for cp in sums:
            cp.wait_recv()
        for route in range(2):
            mine = (y, x)[route]
            lanes = slice(k * 512 + route * 256, k * 512 + route * 256 + 256)
            total = wout[pl.ds(8 + mine * 2, 2), :, span, lanes].reshape(4 * n, 256).astype(F32)
            for d in range(3):
                total = total + rs1[k, route, d, :, :, span, :].reshape(4 * n, 256).astype(F32)
            ag_a[k, :, span, route * 256:(route + 1) * 256] = total.astype(BF).reshape(4, n, 256)
        group = []
        for d in (2, 1, 3):
            xd, yd = (x + d) % 4, (y + d) % 4
            cp_a = remote(
                ag_a.at[k, xd, some, pl.ds(0, 256)],
                rs2.at[d - 1, some, pl.ds(k * 512, 256)],
                r2_s.at[p, 0, d - 1], r2_r.at[p, 0, d - 1], dev(dx=d),
            )
            cp_b = remote(
                ag_a.at[k, yd, some, pl.ds(256, 256)],
                rs2.at[d - 1, some, pl.ds(k * 512 + 256, 256)],
                r2_s.at[p, 1, d - 1], r2_r.at[p, 1, d - 1], dev(dy=d),
            )
            cp_a.start()
            cp_b.start()
            group += [cp_a, cp_b]
        drains.extend(group)
        return group

    def close(p, group):
        k, t0, nt = pieces[p]
        n = nt * 16
        span = slice(t0 * 16, t0 * 16 + n)
        for cp in group:
            cp.wait_recv()
        for route in range(2):
            mine = (x, y)[route]
            total = ag_a[k, mine, span, route * 256:(route + 1) * 256].astype(F32)
            cols = slice(k * 512 + route * 256, k * 512 + (route + 1) * 256)
            for d in range(3):
                total = total + rs2[d, span, cols].astype(F32)
            for i in range(2):
                o_s[k * 4 + route * 2 + i, t0 // 2:(t0 + nt) // 2] = total[
                    :, i * 128:(i + 1) * 128
                ].reshape(nt // 2, 32, 128)

    backs, sums, ends = {}, {}, {}
    for k in range(8):
        if k == 4:
            early = drains[:]
            drains.clear()
        if k < 5:
            backs[k] = down(k)
        if k < 2:
            wait_group(d1[k + 2])
            d2.append(second(2, k + 2))
        if k == 4:
            for cp in early:
                cp.wait_send()
        if 0 <= k - 1 < 5:
            sums[k - 1] = combine(k - 1, backs[k - 1])
        if 0 <= k - 2 < 5:
            ends[k - 2] = halfway(k - 2, sums[k - 2])
        if 0 <= k - 3 < 5:
            close(k - 3, ends[k - 3])

    p_i = lax.broadcasted_iota(jnp.int32, (512, 512), 0)
    o_i = lax.broadcasted_iota(jnp.int32, (512, 512), 1)
    perm = (o_i == ((p_i >> 4) & 7) * 64 + (p_i >> 7) * 16 + (p_i & 15)).astype(F32).astype(BF)
    for g in range(4):
        v = jnp.concatenate(
            [o_s[k * 4 + g].reshape(64, 128) for k in range(4)], axis=1
        )
        hi = v.astype(BF)
        lo = (v - hi.astype(F32)).astype(BF)
        out_ref[:, g * 512:(g + 1) * 512] = (
            resid[:, g * 512:(g + 1) * 512] + dot(hi, perm) + dot(lo, perm)
        ).astype(BF)
    for cp in drains:
        cp.wait_send()


def per_device(
    inputs, cache_keys, cache_values, lengths, new_keys, new_values, queries, out_weight,
    norm_gain, router, experts, master_gate, master_up, master_down,
):
    vm = pl.BlockSpec(memory_space=pltpu.VMEM)
    anyspace = pl.BlockSpec(memory_space=pl.ANY)
    dma = pltpu.SemaphoreType.DMA
    shape5 = (4, 4, 2, 64, 768)
    out = pl.pallas_call(
        kernel,
        out_shape=jax.ShapeDtypeStruct((64, 2048), BF),
        in_specs=[vm] * 6 + [pl.BlockSpec(memory_space=pltpu.SMEM)] + [anyspace] * 7,
        out_specs=vm,
        scratch_shapes=[
            pltpu.VMEM((16, 128, 256), BF),
            pltpu.VMEM((16, 128, 256), BF),
            pltpu.VMEM((2048, 128), BF),
            pltpu.VMEM((DEPTH, 2, 64, 768), F32),
            pltpu.VMEM((3, 4, 4, 2, 64, 768), BF),
            pltpu.VMEM((3, 4, 2, 4, 64, 384), BF),
            pltpu.VMEM((3, 4, 2, 4, 64, 384), BF),
            pltpu.VMEM((2, 4, 4, 2, 64, 768), BF),
            pltpu.VMEM((4, 4, 4, 2, 16, 768), BF),
            pltpu.VMEM((16, 2, 64, 2048), BF),
            pltpu.VMEM((4, 4, 64, 1152), BF),
            pltpu.VMEM((4, 4, 64, 1024), BF),
            pltpu.VMEM((8, 2, 64, 2048), BF),
            pltpu.VMEM((8, 2, 64, 2048), BF),
            pltpu.VMEM((16, 2, 32, 128), F32),
            pltpu.VMEM((16, 8, 256), F32),
            pltpu.VMEM((16, 8, 256), F32),
            pltpu.VMEM((64, 2048), BF),
            pltpu.VMEM((4, 64, 512), BF),
            pltpu.VMEM((64, 2048), F32),
            pltpu.VMEM((4, 256, 256), BF),
            pltpu.VMEM((4, 2, 3, 2, 2, 64, 256), BF),
            pltpu.VMEM((3, 64, 2048), BF),
            dma((DEPTH,)),
            dma((3,)), dma((2, 2, 8)), dma((2, 2, 8)), dma((4, 2, 8)), dma((4, 2, 8)),
            dma((2, 2, 4)), dma((2, 2, 4)),
            dma((4, 2, 4)), dma((4, 2, 4)),
            dma, dma((3,)), dma((3,)), dma((4, 3)), dma((4, 3)), dma,
            dma((4, 4, 4)), dma((4, 4, 4)),
            dma((4, 8)), dma((4, 8)),
            dma((5, 8)), dma((5, 8)),
            dma((5, 2, 3)), dma((5, 2, 3)),
            dma((5, 2, 3)), dma((5, 2, 3)),
        ],
        compiler_params=pltpu.CompilerParams(
            collective_id=0, has_side_effects=True, vmem_limit_bytes=66_900_000
        ),
        name="moe_decode",
    )(
        inputs.reshape(64, 2048), queries, new_keys, new_values,
        norm_gain, experts.transpose(0, 2, 1), lengths, cache_keys, cache_values, router,
        out_weight.reshape(4, 2, 64, 2048),
        master_gate.reshape(shape5), master_up.reshape(shape5), master_down.reshape(shape5),
    )
    return out.reshape(4, 16, 2048)


def solution(mesh):
    return jax.shard_map(
        per_device,
        mesh=mesh,
        in_specs=(
            P(None, ("fsdp", "expert"), None),
            P(("fsdp", "expert"), None, None),
            P(("fsdp", "expert"), None, None),
            P(("fsdp", "expert")),
            P(None, ("fsdp", "expert"), None),
            P(None, ("fsdp", "expert"), None),
            P(None, ("fsdp", "expert"), None),
            P("fsdp", None),
            P(),
            P(),
            P(None, ("fsdp", "expert"), None),
            P("fsdp", "expert", None),
            P("fsdp", "expert", None),
            P("fsdp", "expert", None),
        ),
        out_specs=P(None, ("fsdp", "expert"), None),
        check_vma=False,
    )
```
